32 devices in a mesh: grp: 4 (over x, core), dev: 8 (over z, y).
Axes of the slice: x: 2, y: 2, z: 4, core: 2. Of those that a mesh axis runs over, the one named last changes fastest.
Arguments:
- home_points: bfloat16 [65536, 512], P(('grp', 'dev')), may hold values from -6 to 6
- counts: int32 [32], P(('grp', 'dev')), may hold values from 0 to 2, as said below
- owner_group: int32 [64], P(('grp', 'dev')), may hold values from 0 to 3, as said below
- neighbors_home: int32 [27, 65536], P(None, ('grp', 'dev')), may hold values from 0 to 1023
- hilbert_target: int32 [512], P(('grp', 'dev')), may hold values from 0 to 127, as said below
- neighbors_second: int32 [27, 32768], P(None, ('grp', 'dev')), may hold values from 0 to 1023
- depth_first: float32 [27, 512], replicated, may hold values from -1.5 to 1.5
- mixing_first: bfloat16 [512, 512], replicated, may hold values from -0.25 to 0.25
- gain_first: float32 [512], replicated, may hold values from 0.1 to 1.9
- w_qkv_first: bfloat16 [512, 1536], replicated, may hold values from -3 to 3
- w_out_first: bfloat16 [512, 512], replicated, may hold values from -0.25 to 0.25
- depth_second: float32 [27, 512], replicated, may hold values from -1.5 to 1.5
- mixing_second: bfloat16 [512, 512], replicated, may hold values from -0.25 to 0.25
- gain_second: float32 [512], replicated, may hold values from 0.1 to 1.9
- w_qkv_second: bfloat16 [512, 1536], replicated, may hold values from -3 to 3
- w_out_second: bfloat16 [512, 512], replicated, may hold values from -0.25 to 0.25
Outputs:
- encoded_points: bfloat16 [65536, 512], P(('grp', 'dev'))
The draws below stay inside these ranges and needn't reach their ends.
Inputs may be any that keep to these rules, and one draw needn't show every extreme that they name: For each dev index, the counts of its 4 tiles sum to 4. `owner_group`: the live slots of one tile name distinct groups, and for each dev index d and group q exactly one live slot of the tiles with dev index d names q. Dead slots' values are unused. `hilbert_target`: within each group the targets are a permutation of 0 to 127, and at most 2 blocks of one device name the same device (target // 16).
All inputs are finite; a program needn't handle non-finite values.
Results may differ from the reference program's by a relative error of at most 0.025.
Values may be sent and summed in bfloat16 or wider, within the bound.
A program may use at most 128 MiB of HBM per device.

```python
import jax
import jax.numpy as jnp
from jax import lax

WIDTH = 512
HEADS = 8
HEAD_DIM = 64
PATCH = 1024
NEIGHBORS = 27
BLOCK = 64
BLOCKS = 16
SLOTS = 2
HOME_ROWS = 65536
OWNED_ROWS = 32768
N_GRP = 4
N_DEV = 8


def tile_plan(key):
    heavy_key, order_key, owner_key, spare_key = jax.random.split(key, 4)
    heavy = jax.random.randint(heavy_key, (N_DEV, 1), 1, N_GRP // 2 + 1)
    places = jnp.arange(N_GRP)[None, :]
    levels = jnp.where(places < heavy, SLOTS, jnp.where(places < 2 * heavy, 0, 1))
    shuffle = jnp.argsort(jax.random.randint(order_key, (N_DEV, N_GRP), 0, 1 << 20) * N_GRP + places, axis=1)
    tile_count = jnp.take_along_axis(levels, shuffle, axis=1)
    before = jnp.cumsum(tile_count, axis=1) - tile_count
    owner_perm = jnp.argsort(jax.random.randint(owner_key, (N_DEV, N_GRP), 0, 1 << 20) * N_GRP + places, axis=1)
    spots = jnp.minimum(before[:, :, None] + jnp.arange(SLOTS)[None, None, :], N_GRP - 1)
    chosen = jnp.take_along_axis(owner_perm, spots.reshape(N_DEV, N_GRP * SLOTS), axis=1)
    chosen = chosen.reshape(N_DEV, N_GRP, SLOTS)
    filled = jnp.arange(SLOTS)[None, None, :] < tile_count[:, :, None]
    spare = jax.random.randint(spare_key, (N_DEV, N_GRP, SLOTS), 0, N_GRP)
    owners = jnp.where(filled, chosen, spare)
    return (jnp.transpose(tile_count).reshape(-1).astype(jnp.int32), jnp.transpose(owners, (1, 0, 2)).reshape(-1).astype(jnp.int32))


def draw_counts(key, part):
    planned = tile_plan(key)
    return planned[0]


def draw_owner_group(key, part):
    planned = tile_plan(key)
    return planned[1]


def draw_hilbert_target(key, part):
    key = jax.random.fold_in(key, 5)

    def one_group(group):
        group_key = jax.random.fold_in(key, group)
        pool_key, shuffle_key, slot_key = jax.random.split(group_key, 3)
        candidates = jax.random.permutation(pool_key, 2 * N_DEV) % N_DEV
        leader = candidates[0]
        spots = jnp.arange(2 * N_DEV)
        ranked = jnp.argsort(jnp.where(candidates == leader, 2 * N_DEV + spots, spots))
        offsets = jnp.concatenate([jnp.stack([leader, leader]), candidates[ranked[:BLOCKS - 2]]])
        relabel = jax.random.permutation(shuffle_key, N_DEV)
        senders = jnp.arange(N_DEV)[:, None]
        destination = relabel[(senders + offsets[None, :]) % N_DEV]
        scores = jax.random.randint(slot_key, (N_DEV, BLOCKS), 0, 1 << 20) * BLOCKS + jnp.arange(BLOCKS)[None, :]
        layout = jnp.argsort(scores, axis=1)
        position = layout[destination, jnp.arange(BLOCKS)[None, :]]
        return destination * BLOCKS + position
    return jax.vmap(one_group)(jnp.arange(N_GRP)).reshape(-1).astype(jnp.int32)


def projection_draw(key):
    return (jax.random.normal(key, (WIDTH, 3 * WIDTH), jnp.float32) * 1.4 * WIDTH ** (-0.5)).astype(jnp.bfloat16)


def draw_w_qkv_first(key, part):
    key = jax.random.fold_in(key, 21)
    return projection_draw(key)


def draw_w_qkv_second(key, part):
    key = jax.random.fold_in(key, 37)
    return projection_draw(key)


def plant(array, rng, least, largest):
    extent = array.shape
    place = [jax.random.randint(jax.random.fold_in(rng, axis), (), 0, extent[axis]) for axis in range(len(extent))]
    array = array.at[tuple(place)].set(least)
    longest = extent.index(max(extent))
    place[longest] = (place[longest] + 1) % extent[longest]
    return array.at[tuple(place)].set(largest)


def shard_levels(key, extent, cuts, least, largest):
    def one(axis_at, parts):
        heights = jax.random.uniform(jax.random.fold_in(jax.random.fold_in(key, 6), axis_at), (parts,), jnp.float32, least / len(cuts), largest / len(cuts))
        return jnp.repeat(jnp.exp(heights), extent[axis_at] // parts).reshape((-1,) + (1,) * (len(extent) - axis_at - 1))

    loudness = one(*cuts[0])
    for cut in cuts[1:]:
        loudness = loudness * one(*cut)
    return loudness


def bell_draw(own_key, extent, width, reach, cuts=(), kind=jnp.bfloat16):
    entries = jax.random.normal(own_key, extent, jnp.float32) * width
    if len(cuts) > 0:
        entries = shard_levels(own_key, extent, cuts, -0.22, 0.18) * entries
    return jnp.clip(entries, min=-reach, max=reach).astype(kind)


def setup_inputs(seed: int = 0) -> dict:
    key_of = jax.random.split(jax.random.key(seed), 17)
    home_points = bell_draw(key_of[0], (HOME_ROWS, WIDTH), 1.0, 6.0, ((0, 32),))
    counts = draw_counts(jax.random.fold_in(key_of[16], 71), 0)
    owner_group = draw_owner_group(jax.random.fold_in(key_of[16], 71), 0)
    neighbors_home = plant(jax.random.randint(key_of[3], (NEIGHBORS, HOME_ROWS), 0, PATCH), jax.random.fold_in(key_of[3], 1), 0, PATCH - 1).astype(jnp.int32)
    hilbert_target = draw_hilbert_target(jax.random.fold_in(key_of[16], 71), 0)
    neighbors_second = plant(jax.random.randint(key_of[5], (NEIGHBORS, OWNED_ROWS), 0, PATCH), jax.random.fold_in(key_of[5], 1), 0, PATCH - 1).astype(jnp.int32)
    depth_first = bell_draw(key_of[6], (NEIGHBORS, WIDTH), 0.25, 1.5, (), jnp.float32)
    mixing_first = bell_draw(key_of[7], (WIDTH, WIDTH), WIDTH ** -0.5, 0.25)
    gain_first = jnp.clip(1.0 + 0.18 * jax.random.normal(key_of[8], (WIDTH,), jnp.float32), 0.1, 1.9)
    w_qkv_first = draw_w_qkv_first(jax.random.fold_in(key_of[16], 71), 0)
    w_out_first = bell_draw(key_of[10], (WIDTH, WIDTH), WIDTH ** -0.5, 0.25)
    depth_second = bell_draw(key_of[11], (NEIGHBORS, WIDTH), 0.25, 1.5, (), jnp.float32)
    mixing_second = bell_draw(key_of[12], (WIDTH, WIDTH), WIDTH ** -0.5, 0.25)
    gain_second = jnp.clip(1.0 + 0.18 * jax.random.normal(key_of[13], (WIDTH,), jnp.float32), 0.1, 1.9)
    w_qkv_second = draw_w_qkv_second(jax.random.fold_in(key_of[16], 71), 0)
    w_out_second = bell_draw(key_of[15], (WIDTH, WIDTH), WIDTH ** -0.5, 0.25)
    return dict(home_points=home_points, counts=counts, owner_group=owner_group, neighbors_home=neighbors_home, hilbert_target=hilbert_target, neighbors_second=neighbors_second, depth_first=depth_first, mixing_first=mixing_first, gain_first=gain_first, w_qkv_first=w_qkv_first, w_out_first=w_out_first, depth_second=depth_second, mixing_second=mixing_second, gain_second=gain_second, w_qkv_second=w_qkv_second, w_out_second=w_out_second)


epsilon = 1e-05

def encoder_block(features, neighbours, depth, mixing, gain, w_qkv, w_out):
    gathered = jnp.zeros(features.shape, jnp.float32)
    for which in range(NEIGHBORS):
        gathered = gathered + features[neighbours[which]].astype(jnp.float32) * depth[which]
    encoded = gathered.astype(jnp.bfloat16)
    updated = features.astype(jnp.float32) + jnp.dot(encoded, mixing, preferred_element_type=jnp.float32)
    centre = lax.optimization_barrier(jnp.mean(updated, axis=-1, keepdims=True))
    spread = lax.optimization_barrier(jnp.mean((updated - centre) ** 2, axis=-1, keepdims=True))
    normed = ((updated - centre) * lax.rsqrt(spread + epsilon) * gain).astype(jnp.bfloat16)
    project = jnp.dot(normed, w_qkv, preferred_element_type=jnp.float32).astype(jnp.bfloat16)
    pieces = project.astype(jnp.float32).reshape(PATCH, 3, HEADS, HEAD_DIM)
    scores = jnp.einsum('qhd,khd->hqk', pieces[:, 0], pieces[:, 1]) * HEAD_DIM ** (-0.5)
    peaks = lax.optimization_barrier(jnp.max(scores, axis=-1, keepdims=True))
    powers = jnp.exp(scores - peaks)
    totals = lax.optimization_barrier(jnp.sum(powers, axis=-1, keepdims=True))
    weights = (powers / totals).astype(jnp.bfloat16)
    mixed = jnp.einsum('hqk,khd->qhd', weights.astype(jnp.float32), pieces[:, 2])
    mixed = mixed.reshape(PATCH, WIDTH).astype(jnp.bfloat16)
    return (updated + jnp.dot(mixed, w_out, preferred_element_type=jnp.float32)).astype(jnp.bfloat16)

def reference(home_points, counts, owner_group, neighbors_home, hilbert_target, neighbors_second, depth_first, mixing_first, gain_first, w_qkv_first, w_out_first, depth_second, mixing_second, gain_second, w_qkv_second, w_out_second):
    groups = N_GRP
    owners = N_DEV
    points = home_points.reshape(groups, owners, SLOTS, PATCH, WIDTH)
    lists = neighbors_home.reshape(NEIGHBORS, groups, owners, SLOTS, PATCH)
    tile_count = counts.reshape(groups, owners)
    filled = jnp.arange(SLOTS, dtype=jnp.int32)[None, None, :] < tile_count[:, :, None]
    target = owner_group.reshape(groups, owners, SLOTS)
    match = filled[None] & (target[None] == jnp.arange(groups, dtype=jnp.int32)[:, None, None, None])
    labels = jnp.arange(groups, dtype=jnp.int32)[:, None, None] * SLOTS + jnp.arange(SLOTS, dtype=jnp.int32)[None, None, :]
    source = lax.optimization_barrier(jnp.sum(jnp.where(match, labels[None], 0), axis=(1, 3))).astype(jnp.int32)
    column = jnp.arange(owners, dtype=jnp.int32)[None, :]
    owned = points[source // SLOTS, column, source % SLOTS]
    owned_lists = jnp.transpose(lists[:, source // SLOTS, column, source % SLOTS], (1, 2, 0, 3))
    first_params = (depth_first, mixing_first, gain_first, w_qkv_first, w_out_first)
    second_params = (depth_second, mixing_second, gain_second, w_qkv_second, w_out_second)
    section_one = lax.map(lambda pair: encoder_block(pair[0], pair[1], *first_params), (owned.reshape(groups * owners, PATCH, WIDTH), owned_lists.reshape(groups * owners, NEIGHBORS, PATCH)))
    blocks_one = section_one.reshape(groups, owners * BLOCKS, BLOCK, WIDTH)
    order = hilbert_target.reshape(groups, owners * BLOCKS)
    rowsel = jnp.arange(groups, dtype=jnp.int32)[:, None]
    numbering = jnp.broadcast_to(jnp.arange(owners * BLOCKS, dtype=jnp.int32)[None, :], (groups, owners * BLOCKS))
    inverse = jnp.zeros((groups, owners * BLOCKS), jnp.int32).at[rowsel, order].set(numbering)
    regrouped = blocks_one[rowsel, inverse].reshape(groups * owners, PATCH, WIDTH)
    second_lists = jnp.transpose(neighbors_second.reshape(NEIGHBORS, groups * owners, PATCH), (1, 0, 2))
    section_two = lax.map(lambda pair: encoder_block(pair[0], pair[1], *second_params), (regrouped, second_lists))
    returned = section_two.reshape(groups, owners * BLOCKS, BLOCK, WIDTH)[rowsel, order]
    returned = returned.reshape(groups, owners, PATCH, WIDTH)
    homed = returned[target, jnp.arange(owners, dtype=jnp.int32)[None, :, None]]
    result = jnp.where(filled[:, :, :, None, None], homed, jnp.zeros((), jnp.bfloat16))
    return result.reshape(groups * owners * SLOTS * PATCH, WIDTH)
```

```python
import functools
import math

import jax
import jax.numpy as jnp
from jax import lax
from jax.experimental import pallas as pl
from jax.experimental.pallas import tpu as pltpu
from jax.sharding import PartitionSpec as P

HEADS = 8
HEAD_DIM = 64
CAPACITY = 2
CORES = 2
CHUNK = 256
EPSILON = 1e-05
ONES = 16


def block_kernel(
    fetch_ref,
    order_ref,
    source_ref,
    lists_ref,
    depth_ref,
    mixing_ref,
    gain_ref,
    qkv_ref,
    out_w_ref,
    out_ref,
    x_ref,
    xt_ref,
    wide_ref,
    acc_ref,
    code_ref,
    updated_ref,
    qt_ref,
    k_ref,
    vt_ref,
    mixed_ref,
    result_ref,
):
    rows, width = x_ref.shape
    fanout = depth_ref.shape[1]
    in_blocks = fetch_ref.shape[0]
    out_blocks = order_ref.shape[0]
    piece = rows // in_blocks
    chunks = rows // CHUNK
    for b in range(in_blocks):
        x_ref[pl.ds(b * piece, piece), :] = source_ref[
            pl.ds(pl.multiple_of(fetch_ref[b] * piece, piece), piece), :
        ]
    xt_ref[...] = x_ref[...].T
    for j in range(fanout):
        wide_ref[j] = jnp.broadcast_to(depth_ref[:, j : j + 1], (width, 128))
    places = lax.broadcasted_iota(jnp.int32, (rows, CHUNK), 0).astype(jnp.int16)

    @pl.loop(0, chunks)
    def _(c):
        at = pl.multiple_of(c * CHUNK, CHUNK)
        acc_ref[...] = jnp.zeros_like(acc_ref)

        @pl.loop(0, fanout, step=3)
        def _(j0):
            total = acc_ref[...]
            for dj in range(3):
                j = j0 + dj
                row = lists_ref[pl.ds(j, 1), pl.ds(at, CHUNK)].astype(jnp.int16)
                hot = jnp.where(places == row, 1.0, 0.0).astype(jnp.bfloat16)
                got = jnp.dot(xt_ref[...], hot, preferred_element_type=jnp.float32)
                weight = wide_ref[j]
                total = total + got * jnp.concatenate([weight] * (CHUNK // 128), axis=1)
            acc_ref[...] = total

        code_ref[pl.ds(at, CHUNK), :] = acc_ref[...].T.astype(jnp.bfloat16)

    gain = gain_ref[...]
    scale = HEAD_DIM**-0.5 * math.log2(math.e)

    @pl.loop(0, chunks)
    def _(c):
        here = pl.ds(pl.multiple_of(c * CHUNK, CHUNK), CHUNK)
        updated = x_ref[here, :].astype(jnp.float32) + jnp.dot(
            code_ref[here, :], mixing_ref[...], preferred_element_type=jnp.float32
        )
        updated_ref[here, :] = updated
        centre = jnp.mean(updated, axis=-1, keepdims=True)
        moved = updated - centre
        spread = jnp.mean(moved * moved, axis=-1, keepdims=True)
        normed = (moved * lax.rsqrt(spread + EPSILON) * gain).astype(jnp.bfloat16)
        project = jnp.dot(normed, qkv_ref[...], preferred_element_type=jnp.float32)
        qt_ref[:, here] = (project[:, :width] * scale).T.astype(jnp.bfloat16)
        k_ref[here, :] = project[:, width : 2 * width].astype(jnp.bfloat16)
        values = project[:, 2 * width :].T.astype(jnp.bfloat16)
        for h in range(HEADS):
            vt_ref[h, :HEAD_DIM, here] = values[h * HEAD_DIM : (h + 1) * HEAD_DIM]

    vt_ref[:, HEAD_DIM:, :] = jnp.ones((HEADS, ONES, rows), jnp.bfloat16)

    @pl.loop(0, chunks)
    def _(c):
        here = pl.ds(pl.multiple_of(c * CHUNK, CHUNK), CHUNK)
        for h in range(HEADS):
            pair = h // 2
            zero = jnp.zeros((HEAD_DIM, CHUNK), jnp.bfloat16)
            query = qt_ref[pl.ds(h * HEAD_DIM, HEAD_DIM), here]
            padded = jnp.concatenate([query, zero] if h % 2 == 0 else [zero, query], axis=0)
            scores = jnp.dot(
                k_ref[:, pair * 128 : (pair + 1) * 128], padded, preferred_element_type=jnp.float32
            )
            peak = jnp.max(scores, axis=0, keepdims=True)
            powers = jnp.exp2(scores - peak).astype(jnp.bfloat16)
            mixed = jnp.dot(vt_ref[h], powers, preferred_element_type=jnp.float32)
            mixed_ref[pl.ds(h * HEAD_DIM, HEAD_DIM), :] = (
                mixed[:HEAD_DIM] / mixed[HEAD_DIM : HEAD_DIM + 1]
            )
        mixed = mixed_ref[...].T.astype(jnp.bfloat16)
        result_ref[here, :] = (
            updated_ref[here, :]
            + jnp.dot(mixed, out_w_ref[...], preferred_element_type=jnp.float32)
        ).astype(jnp.bfloat16)

    for b in range(out_blocks):
        out_ref[pl.ds(b * piece, piece), :] = result_ref[
            pl.ds(pl.multiple_of(order_ref[b] * piece, piece), piece), :
        ]


def run_block(source, lists, params, fetch, order, rows):
    depth, mixing, gain, w_qkv, w_out = params
    width = source.shape[1]
    fanout = lists.shape[0]
    piece = rows // fetch.shape[0]
    vmem = pl.BlockSpec(memory_space=pltpu.VMEM)
    smem = pl.BlockSpec(memory_space=pltpu.SMEM)
    return pl.pallas_call(
        block_kernel,
        out_shape=jax.ShapeDtypeStruct((order.shape[0] * piece, width), jnp.bfloat16),
        in_specs=[smem, smem] + [vmem] * 7,
        out_specs=vmem,
        scratch_shapes=[
            pltpu.VMEM((rows, width), jnp.bfloat16),
            pltpu.VMEM((width, rows), jnp.bfloat16),
            pltpu.VMEM((fanout, width, 128), jnp.float32),
            pltpu.VMEM((width, CHUNK), jnp.float32),
            pltpu.VMEM((rows, width), jnp.bfloat16),
            pltpu.VMEM((rows, width), jnp.float32),
            pltpu.VMEM((width, rows), jnp.bfloat16),
            pltpu.VMEM((rows, width), jnp.bfloat16),
            pltpu.VMEM((HEADS, HEAD_DIM + ONES, rows), jnp.bfloat16),
            pltpu.VMEM((width, CHUNK), jnp.float32),
            pltpu.VMEM((rows, width), jnp.bfloat16),
        ],
        compiler_params=pltpu.CompilerParams(vmem_limit_bytes=56 * 1024 * 1024),
        cost_estimate=pl.CostEstimate(
            flops=2 * fanout * rows * rows * width, bytes_accessed=8 << 20, transcendentals=8 << 20
        ),
        name="block",
    )(fetch, order, source, lists, depth.T, mixing, gain.reshape(1, width), w_qkv, w_out)


def body(
    home_points,
    counts,
    owner_group,
    neighbors_home,
    hilbert_target,
    neighbors_second,
    depth_first,
    mixing_first,
    gain_first,
    w_qkv_first,
    w_out_first,
    depth_second,
    mixing_second,
    gain_second,
    w_qkv_second,
    w_out_second,
):
    groups = lax.axis_size("grp")
    owners = lax.axis_size("dev")
    chips = groups // CORES
    me = lax.axis_index("grp")
    place_x, core = me // CORES, me % CORES
    mine = lax.axis_index("dev")
    home_rows, width = home_points.shape
    slot_count = owner_group.shape[0]
    rows = home_rows // slot_count
    block_count = hilbert_target.shape[0]
    piece = rows // block_count
    fanout = neighbors_home.shape[0]
    mate = [(i, i ^ 1) for i in range(groups)]
    first_params = (depth_first, mixing_first, gain_first, w_qkv_first, w_out_first)
    second_params = (depth_second, mixing_second, gain_second, w_qkv_second, w_out_second)

    targets = lax.all_gather(hilbert_target, "dev", axis=0, tiled=True).reshape(
        owners, block_count
    )

    filled = jnp.arange(slot_count) < counts[0]
    wanted = jnp.where(filled, owner_group, -1)
    tiles = home_points.reshape(slot_count, rows, width)
    lists = jnp.transpose(neighbors_home.reshape(fanout, slot_count, rows), (1, 0, 2))
    stamped = jnp.concatenate(
        [lists, jnp.broadcast_to(wanted[:, None, None], (slot_count, 1, rows))], axis=1
    )
    other_tiles = lax.ppermute(tiles, "grp", mate)
    other_stamped = lax.ppermute(stamped, "grp", mate)
    other_wanted = other_stamped[:, fanout, 0]

    def candidate(target):
        here, there = wanted == target, other_wanted == target
        at_here = jnp.sum(jnp.where(here, jnp.arange(slot_count), 0))
        at_there = jnp.sum(jnp.where(there, jnp.arange(slot_count), 0))
        ours = jnp.any(here)
        pick = lambda a, b: jnp.where(
            ours,
            lax.dynamic_index_in_dim(a, at_here, 0, keepdims=False),
            lax.dynamic_index_in_dim(b, at_there, 0, keepdims=False),
        )
        return ours | jnp.any(there), pick(tiles, other_tiles), pick(stamped, other_stamped)

    held, points, stamps = candidate(me)
    for r in range(1, chips):
        target = ((place_x + r) % chips) * CORES + core
        _, points_out, stamps_out = candidate(target)
        over = [
            (x * CORES + c, ((x + r) % chips) * CORES + c)
            for x in range(chips)
            for c in range(CORES)
        ]
        points_in = lax.ppermute(points_out, "grp", over)
        stamps_in = lax.ppermute(stamps_out, "grp", over)
        take = stamps_in[fanout, 0] == me
        points = jnp.where(take, points_in, points)
        stamps = jnp.where(take, stamps_in, stamps)

    slots = owners * CAPACITY
    counter = jnp.arange(block_count)
    destination = targets // block_count
    same = destination[:, :, None] == destination[:, None, :]
    rank = jnp.sum(same & (counter[:, None] > counter[None, :]), axis=2)
    places = destination * CAPACITY + rank
    place = lax.dynamic_index_in_dim(places, mine, 0, keepdims=False)
    order = jnp.sum(
        jnp.where(place[None, :] == jnp.arange(slots)[:, None], counter[None, :], 0), axis=1
    ).astype(jnp.int32)
    sent_at = (jnp.arange(owners)[:, None] * CAPACITY + rank).reshape(-1)
    flat = targets.reshape(-1)
    goal = mine * block_count + counter
    fetch = jnp.sum(
        jnp.where(flat[None, :] == goal[:, None], sent_at[None, :], 0), axis=1
    ).astype(jnp.int32)
    back = jnp.sum(
        jnp.where(fetch[None, :] == jnp.arange(slots)[:, None], counter[None, :], 0), axis=1
    ).astype(jnp.int32)

    straight = jnp.arange(block_count, dtype=jnp.int32)
    outgoing = run_block(points, stamps[:fanout], first_params, straight, order, rows)
    swap = lambda a: lax.all_to_all(a, "dev", split_axis=0, concat_axis=0, tiled=True)
    incoming = swap(outgoing)
    backward = run_block(incoming, neighbors_second, second_params, fetch, back, rows)
    returned = swap(backward).reshape(slots, piece, width)
    finished = returned[place].reshape(rows, width)

    gathered = [finished]
    for r in range(1, chips):
        over = [
            (x * CORES + c, ((x + r) % chips) * CORES + c)
            for x in range(chips)
            for c in range(CORES)
        ]
        gathered.append(lax.ppermute(finished, "grp", over))
    stack = jnp.stack(gathered)
    other = lax.ppermute(stack, "grp", mate)
    shift = (place_x - owner_group // CORES) % chips
    ours = owner_group % CORES == core
    parts = [
        jnp.where(
            filled[s],
            jnp.where(
                ours[s],
                lax.dynamic_index_in_dim(stack, shift[s], 0, keepdims=False),
                lax.dynamic_index_in_dim(other, shift[s], 0, keepdims=False),
            ),
            jnp.zeros((), jnp.bfloat16),
        )
        for s in range(slot_count)
    ]
    return jnp.concatenate(parts, axis=0)


def solution(mesh):
    return jax.shard_map(
        body,
        mesh=mesh,
        in_specs=(
            P(("grp", "dev"), None),
            P(("grp", "dev")),
            P(("grp", "dev")),
            P(None, ("grp", "dev")),
            P(("grp", "dev")),
            P(None, ("grp", "dev")),
            P(),
            P(),
            P(),
            P(),
            P(),
            P(),
            P(),
            P(),
            P(),
            P(),
        ),
        out_specs=P(("grp", "dev"), None),
        check_vma=False,
    )
```

```python
import functools
import math

import jax
import jax.numpy as jnp
from jax import lax
from jax.experimental import pallas as pl
from jax.experimental.pallas import tpu as pltpu
from jax.sharding import PartitionSpec as P

HEADS = 8
HEAD_DIM = 64
CAPACITY = 2
CORES = 2
CHUNK = 256
EPSILON = 1e-05
ONES = 16
PRODUCTS = 12
STEP = 3


def block_kernel(
    fetch_ref,
    order_ref,
    near_ref,
    source_ref,
    lists_ref,
    depth_ref,
    turned_ref,
    mixing_ref,
    gain_ref,
    qkv_ref,
    out_w_ref,
    out_ref,
    x_ref,
    xt_ref,
    fine_ref,
    slim_ref,
    sums_ref,
    wide_ref,
    acc_ref,
    code_ref,
    updated_ref,
    qt_ref,
    k_ref,
    vt_ref,
    mixed_ref,
    result_ref,
):
    rows, width = x_ref.shape
    fanout = depth_ref.shape[0]
    in_blocks = fetch_ref.shape[0]
    out_blocks = order_ref.shape[0]
    piece = rows // in_blocks
    chunks = rows // CHUNK
    lanes = 128
    parts = width // lanes
    for b in range(in_blocks):
        x_ref[pl.ds(b * piece, piece), :] = source_ref[
            pl.ds(pl.multiple_of(fetch_ref[b] * piece, piece), piece), :
        ]
    xt_ref[...] = x_ref[...].T
    for c in range(parts):
        fine_ref[pl.ds(c, rows, stride=parts), :] = x_ref[:, c * lanes : (c + 1) * lanes].astype(
            jnp.float32
        )
        slim_ref[pl.ds(c, fanout, stride=parts), :] = depth_ref[:, c * lanes : (c + 1) * lanes]
    for j in range(PRODUCTS):
        wide_ref[j] = jnp.broadcast_to(turned_ref[:, j : j + 1], (width, lanes))
    places = (lax.broadcasted_iota(jnp.int32, (rows, CHUNK), 0) * parts).astype(jnp.int16)
    one, nil = jnp.bfloat16(1), jnp.bfloat16(0)
    turns = PRODUCTS // STEP
    points = CHUNK // turns

    @pl.loop(0, chunks)
    def _(c):
        at = pl.multiple_of(c * CHUNK, CHUNK)
        acc_ref[...] = jnp.zeros_like(acc_ref)

        @pl.loop(0, turns)
        def _(t):
            total = acc_ref[...]
            for dj in range(STEP):
                j = t * STEP + dj
                row = lists_ref[pl.ds(j, 1), pl.ds(at, CHUNK)].astype(jnp.int16)
                hot = jnp.where(places == row, one, nil)
                got = jnp.dot(xt_ref[...], hot, preferred_element_type=jnp.float32)
                weight = wide_ref[j]
                total = total + got * jnp.concatenate([weight] * (CHUNK // lanes), axis=1)
            acc_ref[...] = total
            first = t * points
            weights = [slim_ref[pl.ds(j * parts, parts), :] for j in range(PRODUCTS, fanout)]
            for p in range(points):
                total = None
                for j in range(PRODUCTS, fanout):
                    line = pl.multiple_of(near_ref[j, at + first + p], parts)
                    term = fine_ref[pl.ds(line, parts), :] * weights[j - PRODUCTS]
                    total = term if total is None else total + term
                sums_ref[pl.ds(pl.multiple_of((first + p) * parts, parts), parts), :] = total

        for i in range(parts):
            code_ref[pl.ds(at, CHUNK), i * lanes : (i + 1) * lanes] = (
                acc_ref[i * lanes : (i + 1) * lanes, :].T
                + sums_ref[pl.ds(i, CHUNK, stride=parts), :]
            ).astype(jnp.bfloat16)

    gain = gain_ref[...]
    scale = HEAD_DIM**-0.5 * math.log2(math.e)

    @pl.loop(0, chunks)
    def _(c):
        here = pl.ds(pl.multiple_of(c * CHUNK, CHUNK), CHUNK)
        updated = x_ref[here, :].astype(jnp.float32) + jnp.dot(
            code_ref[here, :], mixing_ref[...], preferred_element_type=jnp.float32
        )
        updated_ref[here, :] = updated
        centre = jnp.mean(updated, axis=-1, keepdims=True)
        moved = updated - centre
        spread = jnp.mean(moved * moved, axis=-1, keepdims=True)
        normed = (moved * lax.rsqrt(spread + EPSILON) * gain).astype(jnp.bfloat16)
        project = jnp.dot(normed, qkv_ref[...], preferred_element_type=jnp.float32)
        qt_ref[:, here] = (project[:, :width] * scale).T.astype(jnp.bfloat16)
        k_ref[here, :] = project[:, width : 2 * width].astype(jnp.bfloat16)
        values = project[:, 2 * width :].T.astype(jnp.bfloat16)
        for h in range(HEADS):
            vt_ref[h, :HEAD_DIM, here] = values[h * HEAD_DIM : (h + 1) * HEAD_DIM]

    vt_ref[:, HEAD_DIM:, :] = jnp.ones((HEADS, ONES, rows), jnp.bfloat16)

    @pl.loop(0, chunks)
    def _(c):
        here = pl.ds(pl.multiple_of(c * CHUNK, CHUNK), CHUNK)

        def scored(h):
            pair = h // 2
            zero = jnp.zeros((HEAD_DIM, CHUNK), jnp.bfloat16)
            query = qt_ref[pl.ds(h * HEAD_DIM, HEAD_DIM), here]
            padded = jnp.concatenate([query, zero] if h % 2 == 0 else [zero, query], axis=0)
            return jnp.dot(
                k_ref[:, pair * lanes : (pair + 1) * lanes],
                padded,
                preferred_element_type=jnp.float32,
            )

        scores = scored(0)
        for h in range(HEADS):
            following = scored(h + 1) if h + 1 < HEADS else None
            peak = jnp.max(scores, axis=0, keepdims=True)
            powers = jnp.exp2(scores - peak).astype(jnp.bfloat16)
            mixed = jnp.dot(vt_ref[h], powers, preferred_element_type=jnp.float32)
            mixed_ref[pl.ds(h * HEAD_DIM, HEAD_DIM), :] = (
                mixed[:HEAD_DIM] / mixed[HEAD_DIM : HEAD_DIM + 1]
            )
            scores = following
        mixed = mixed_ref[...].T.astype(jnp.bfloat16)
        result_ref[here, :] = (
            updated_ref[here, :]
            + jnp.dot(mixed, out_w_ref[...], preferred_element_type=jnp.float32)
        ).astype(jnp.bfloat16)

    for b in range(out_blocks):
        out_ref[pl.ds(b * piece, piece), :] = result_ref[
            pl.ds(pl.multiple_of(order_ref[b] * piece, piece), piece), :
        ]


def run_block(source, lines, params, fetch, order, rows):
    depth, mixing, gain, w_qkv, w_out = params
    width = source.shape[1]
    fanout = lines.shape[0]
    piece = rows // fetch.shape[0]
    parts = width // 128
    vmem = pl.BlockSpec(memory_space=pltpu.VMEM)
    smem = pl.BlockSpec(memory_space=pltpu.SMEM)
    return pl.pallas_call(
        block_kernel,
        out_shape=jax.ShapeDtypeStruct((order.shape[0] * piece, width), jnp.bfloat16),
        in_specs=[smem] * 3 + [vmem] * 8,
        out_specs=vmem,
        scratch_shapes=[
            pltpu.VMEM((rows, width), jnp.bfloat16),
            pltpu.VMEM((width, rows), jnp.bfloat16),
            pltpu.VMEM((rows * parts, 128), jnp.float32),
            pltpu.VMEM((fanout * parts, 128), jnp.float32),
            pltpu.VMEM((CHUNK * parts, 128), jnp.float32),
            pltpu.VMEM((PRODUCTS, width, 128), jnp.float32),
            pltpu.VMEM((width, CHUNK), jnp.float32),
            pltpu.VMEM((rows, width), jnp.bfloat16),
            pltpu.VMEM((rows, width), jnp.float32),
            pltpu.VMEM((width, rows), jnp.bfloat16),
            pltpu.VMEM((rows, width), jnp.bfloat16),
            pltpu.VMEM((HEADS, HEAD_DIM + ONES, rows), jnp.bfloat16),
            pltpu.VMEM((width, CHUNK), jnp.float32),
            pltpu.VMEM((rows, width), jnp.bfloat16),
        ],
        compiler_params=pltpu.CompilerParams(vmem_limit_bytes=56 * 1024 * 1024),
        cost_estimate=pl.CostEstimate(
            flops=2 * fanout * rows * rows * width, bytes_accessed=8 << 20, transcendentals=8 << 20
        ),
        name="block",
    )(
        fetch,
        order,
        lines,
        source,
        lines,
        depth,
        depth.T,
        mixing,
        gain.reshape(1, width),
        w_qkv,
        w_out,
    )


def body(
    home_points,
    counts,
    owner_group,
    neighbors_home,
    hilbert_target,
    neighbors_second,
    depth_first,
    mixing_first,
    gain_first,
    w_qkv_first,
    w_out_first,
    depth_second,
    mixing_second,
    gain_second,
    w_qkv_second,
    w_out_second,
):
    groups = lax.axis_size("grp")
    owners = lax.axis_size("dev")
    chips = groups // CORES
    me = lax.axis_index("grp")
    place_x, core = me // CORES, me % CORES
    mine = lax.axis_index("dev")
    home_rows, width = home_points.shape
    slot_count = owner_group.shape[0]
    rows = home_rows // slot_count
    block_count = hilbert_target.shape[0]
    piece = rows // block_count
    fanout = neighbors_home.shape[0]
    mate = [(i, i ^ 1) for i in range(groups)]
    first_params = (depth_first, mixing_first, gain_first, w_qkv_first, w_out_first)
    second_params = (depth_second, mixing_second, gain_second, w_qkv_second, w_out_second)

    targets = lax.all_gather(hilbert_target, "dev", axis=0, tiled=True).reshape(
        owners, block_count
    )

    filled = jnp.arange(slot_count) < counts[0]
    wanted = jnp.where(filled, owner_group, -1)
    tiles = home_points.reshape(slot_count, rows, width)
    lists = jnp.transpose(neighbors_home.reshape(fanout, slot_count, rows), (1, 0, 2))
    stamped = jnp.concatenate(
        [lists, jnp.broadcast_to(wanted[:, None, None], (slot_count, 1, rows))], axis=1
    )
    other_tiles = lax.ppermute(tiles, "grp", mate)
    other_stamped = lax.ppermute(stamped, "grp", mate)
    other_wanted = other_stamped[:, fanout, 0]

    def candidate(target):
        here, there = wanted == target, other_wanted == target
        at_here = jnp.sum(jnp.where(here, jnp.arange(slot_count), 0))
        at_there = jnp.sum(jnp.where(there, jnp.arange(slot_count), 0))
        ours = jnp.any(here)
        pick = lambda a, b: jnp.where(
            ours,
            lax.dynamic_index_in_dim(a, at_here, 0, keepdims=False),
            lax.dynamic_index_in_dim(b, at_there, 0, keepdims=False),
        )
        return ours | jnp.any(there), pick(tiles, other_tiles), pick(stamped, other_stamped)

    held, points, stamps = candidate(me)
    for r in range(1, chips):
        target = ((place_x + r) % chips) * CORES + core
        _, points_out, stamps_out = candidate(target)
        over = [
            (x * CORES + c, ((x + r) % chips) * CORES + c)
            for x in range(chips)
            for c in range(CORES)
        ]
        points_in = lax.ppermute(points_out, "grp", over)
        stamps_in = lax.ppermute(stamps_out, "grp", over)
        take = stamps_in[fanout, 0] == me
        points = jnp.where(take, points_in, points)
        stamps = jnp.where(take, stamps_in, stamps)

    slots = owners * CAPACITY
    counter = jnp.arange(block_count)
    destination = targets // block_count
    same = destination[:, :, None] == destination[:, None, :]
    rank = jnp.sum(same & (counter[:, None] > counter[None, :]), axis=2)
    places = destination * CAPACITY + rank
    place = lax.dynamic_index_in_dim(places, mine, 0, keepdims=False)
    order = jnp.sum(
        jnp.where(place[None, :] == jnp.arange(slots)[:, None], counter[None, :], 0), axis=1
    ).astype(jnp.int32)
    sent_at = (jnp.arange(owners)[:, None] * CAPACITY + rank).reshape(-1)
    flat = targets.reshape(-1)
    goal = mine * block_count + counter
    fetch = jnp.sum(
        jnp.where(flat[None, :] == goal[:, None], sent_at[None, :], 0), axis=1
    ).astype(jnp.int32)
    back = jnp.sum(
        jnp.where(fetch[None, :] == jnp.arange(slots)[:, None], counter[None, :], 0), axis=1
    ).astype(jnp.int32)

    straight = jnp.arange(block_count, dtype=jnp.int32)
    outgoing = run_block(points, stamps[:fanout] * (width // 128), first_params, straight, order, rows)
    swap = lambda a: lax.all_to_all(a, "dev", split_axis=0, concat_axis=0, tiled=True)
    incoming = swap(outgoing)
    backward = run_block(incoming, neighbors_second * (width // 128), second_params, fetch, back, rows)
    returned = swap(backward).reshape(slots, piece, width)
    finished = returned[place].reshape(rows, width)

    gathered = [finished]
    for r in range(1, chips):
        over = [
            (x * CORES + c, ((x + r) % chips) * CORES + c)
            for x in range(chips)
            for c in range(CORES)
        ]
        gathered.append(lax.ppermute(finished, "grp", over))
    stack = jnp.stack(gathered)
    other = lax.ppermute(stack, "grp", mate)
    shift = (place_x - owner_group // CORES) % chips
    ours = owner_group % CORES == core
    parts = [
        jnp.where(
            filled[s],
            jnp.where(
                ours[s],
                lax.dynamic_index_in_dim(stack, shift[s], 0, keepdims=False),
                lax.dynamic_index_in_dim(other, shift[s], 0, keepdims=False),
            ),
            jnp.zeros((), jnp.bfloat16),
        )
        for s in range(slot_count)
    ]
    return jnp.concatenate(parts, axis=0)


def solution(mesh):
    return jax.shard_map(
        body,
        mesh=mesh,
        in_specs=(
            P(("grp", "dev"), None),
            P(("grp", "dev")),
            P(("grp", "dev")),
            P(None, ("grp", "dev")),
            P(("grp", "dev")),
            P(None, ("grp", "dev")),
            P(),
            P(),
            P(),
            P(),
            P(),
            P(),
            P(),
            P(),
            P(),
            P(),
        ),
        out_specs=P(("grp", "dev"), None),
        check_vma=False,
    )
```

```python
import functools
import math

import jax
import jax.numpy as jnp
from jax import lax
from jax.experimental import pallas as pl
from jax.experimental.pallas import tpu as pltpu
from jax.sharding import PartitionSpec as P

HEADS = 8
HEAD_DIM = 64
CAPACITY = 2
CORES = 2
CHUNK = 256
EPSILON = 1e-05
ONES = 16
PRODUCTS = 12
STEP = 3
LIMIT = 56 * 1024 * 1024


MESH = pl.DeviceIdType.MESH


def around(size, at, step):
    return lax.rem(at + step + size, size)


def greet(peers):
    barrier = pltpu.get_barrier_semaphore()
    for peer in peers:
        pl.semaphore_signal(barrier, inc=1, device_id=peer, device_id_type=MESH)
    return lambda: pl.semaphore_wait(barrier, len(peers))


def neighbours_of(groups, owners):
    me, mine = lax.axis_index("grp"), lax.axis_index("dev")
    chip, core = me // CORES, lax.rem(me, CORES)
    mate = (chip * CORES + 1 - core, mine)
    over = ((1 - chip) * CORES + core, mine)
    slant = ((1 - chip) * CORES + 1 - core, mine)
    return mate, over, slant


def owners_kernel(
    owners,
    points_ref,
    lists_ref,
    meta_ref,
    points_out,
    lists_out,
    metas_out,
    mate_points,
    mate_lists,
    out_points,
    out_lists,
    in_points,
    in_lists,
    metas_ref,
    meta_send,
    meta_recv,
    mate_send,
    mate_recv,
    over_send,
    over_recv,
):
    me, mine = lax.axis_index("grp"), lax.axis_index("dev")
    rows = points_out.shape[0]
    half = rows // 2
    mate, over, slant = neighbours_of(4, owners)
    column = [mate, over, slant]
    line = [(me, around(owners, mine, k)) for k in range(1, owners)]
    peers = column + line
    entered = greet(peers)
    entered()

    def meta_copy(i, slot):
        return pltpu.make_async_remote_copy(
            meta_ref,
            metas_ref.at[slot],
            meta_send.at[i],
            meta_recv.at[i],
            device_id=peers[i],
            device_id_type=MESH,
        )

    count = len(peers)
    metas = [meta_copy(i, i if i < 3 else i + 1) for i in range(count)]
    for copy in metas:
        copy.start()
    metas_ref[3] = meta_ref[...]

    def mate_copy(i):
        slot, part = i % 2, i // 2
        span = pl.ds(slot * rows + part * half, half)
        return pltpu.make_async_remote_copy(
            points_ref.at[span],
            mate_points.at[span],
            mate_send.at[i],
            mate_recv.at[i],
            device_id=mate,
            device_id_type=MESH,
        )

    moves = [mate_copy(i) for i in range(4)]
    moves.append(
        pltpu.make_async_remote_copy(
            lists_ref,
            mate_lists,
            mate_send.at[4],
            mate_recv.at[4],
            device_id=mate,
            device_id_type=MESH,
        )
    )
    for i in (4, 0, 1, 2, 3):
        moves[i].start()
    for copy in metas:
        copy.wait_recv()

    def flags(target):
        return [
            meta_ref[0:1, :] == target,
            meta_ref[1:2, :] == target,
            metas_ref[0, 0:1, :] == target,
            metas_ref[0, 1:2, :] == target,
        ]

    def chosen_points(target, part):
        total = None
        for flag, (ref, slot) in zip(
            flags(target), [(points_ref, 0), (points_ref, 1), (mate_points, 0), (mate_points, 1)]
        ):
            keep = jnp.where(flag, 1.0, 0.0).astype(jnp.bfloat16)
            term = ref[pl.ds(slot * rows + part * half, half), :] * keep
            total = term if total is None else total + term
        return total

    def chosen_lists(target):
        total = None
        for flag, (ref, slot) in zip(
            flags(target), [(lists_ref, 0), (lists_ref, 1), (mate_lists, 0), (mate_lists, 1)]
        ):
            keep = jnp.where(flag, 1, 0)
            keep = jnp.concatenate([keep] * (rows // keep.shape[1]), axis=1)
            term = ref[:, slot * rows : (slot + 1) * rows] * keep
            total = term if total is None else total + term
        return total

    target = over[0]
    sends = [
        pltpu.make_async_remote_copy(
            source,
            landing,
            over_send.at[i],
            over_recv.at[i],
            device_id=over,
            device_id_type=MESH,
        )
        for i, (source, landing) in enumerate(
            [
                (out_points.at[pl.ds(0, half)], in_points.at[pl.ds(0, half)]),
                (out_points.at[pl.ds(half, half)], in_points.at[pl.ds(half, half)]),
                (out_lists, in_lists),
            ]
        )
    ]
    moves[4].wait_recv()
    out_lists[...] = chosen_lists(target)
    sends[2].start()
    for part in range(2):
        moves[2 * part].wait_recv()
        moves[2 * part + 1].wait_recv()
        out_points[pl.ds(part * half, half), :] = chosen_points(target, part)
        sends[part].start()
    metas_out[...] = metas_ref[...]
    ours = chosen_lists(me)
    for part in range(2):
        points_out[pl.ds(part * half, half), :] = chosen_points(me, part)
    sends[2].wait_recv()
    lists_out[...] = (ours + in_lists[...]) * (points_ref.shape[1] // 128)
    for part in range(2):
        sends[part].wait_recv()
        span = pl.ds(part * half, half)
        points_out[span, :] = points_out[span, :] + in_points[span, :]
    for copy in metas + moves + sends:
        copy.wait_send()


def to_owners(points, lists, meta, owners):
    rows, width = points.shape[0] // 2, points.shape[1]
    fanout = lists.shape[0]
    vmem = pl.BlockSpec(memory_space=pltpu.VMEM)
    count = owners + 2
    return pl.pallas_call(
        functools.partial(owners_kernel, owners),
        out_shape=(
            jax.ShapeDtypeStruct((rows, width), points.dtype),
            jax.ShapeDtypeStruct((fanout, rows), jnp.int32),
            jax.ShapeDtypeStruct((count + 1,) + meta.shape, jnp.int32),
        ),
        in_specs=[vmem] * 3,
        out_specs=(vmem,) * 3,
        scratch_shapes=[
            pltpu.VMEM(points.shape, points.dtype),
            pltpu.VMEM(lists.shape, jnp.int32),
            pltpu.VMEM((rows, width), points.dtype),
            pltpu.VMEM((fanout, rows), jnp.int32),
            pltpu.VMEM((rows, width), points.dtype),
            pltpu.VMEM((fanout, rows), jnp.int32),
            pltpu.VMEM((count + 1,) + meta.shape, jnp.int32),
            pltpu.SemaphoreType.DMA((count,)),
            pltpu.SemaphoreType.DMA((count,)),
            pltpu.SemaphoreType.DMA((5,)),
            pltpu.SemaphoreType.DMA((5,)),
            pltpu.SemaphoreType.DMA((3,)),
            pltpu.SemaphoreType.DMA((3,)),
        ],
        compiler_params=pltpu.CompilerParams(
            collective_id=0, has_side_effects=True, vmem_limit_bytes=56 * 1024 * 1024
        ),
        cost_estimate=pl.CostEstimate(flops=1 << 20, bytes_accessed=8 << 20, transcendentals=0),
        name="to_owners",
    )(points, lists, meta)


def encode_kernel(
    fetch_ref,
    order_ref,
    near_ref,
    source_ref,
    lists_ref,
    depth_ref,
    turned_ref,
    features_ref,
    encoded_ref,
    x_ref,
    xt_ref,
    fine_ref,
    slim_ref,
    sums_ref,
    wide_ref,
    acc_ref,
    code_ref,
):
    rows, width = x_ref.shape
    fanout = depth_ref.shape[0]
    in_blocks = fetch_ref.shape[0]
    piece = rows // in_blocks
    chunks = rows // CHUNK
    lanes = 128
    parts = width // lanes
    for b in range(in_blocks):
        x_ref[pl.ds(b * piece, piece), :] = source_ref[
            pl.ds(pl.multiple_of(fetch_ref[b] * piece, piece), piece), :
        ]
    xt_ref[...] = x_ref[...].T
    for c in range(parts):
        fine_ref[pl.ds(c, rows, stride=parts), :] = x_ref[:, c * lanes : (c + 1) * lanes].astype(
            jnp.float32
        )
        slim_ref[pl.ds(c, fanout, stride=parts), :] = depth_ref[:, c * lanes : (c + 1) * lanes]
    for j in range(PRODUCTS):
        wide_ref[j] = jnp.broadcast_to(turned_ref[:, j : j + 1], (width, lanes))
    places = (lax.broadcasted_iota(jnp.int32, (rows, CHUNK), 0) * parts).astype(jnp.int16)
    one, nil = jnp.bfloat16(1), jnp.bfloat16(0)
    turns = PRODUCTS // STEP
    points = CHUNK // turns

    @pl.loop(0, chunks)
    def _(c):
        at = pl.multiple_of(c * CHUNK, CHUNK)
        acc_ref[...] = jnp.zeros_like(acc_ref)

        @pl.loop(0, turns)
        def _(t):
            total = acc_ref[...]
            for dj in range(STEP):
                j = t * STEP + dj
                row = lists_ref[pl.ds(j, 1), pl.ds(at, CHUNK)].astype(jnp.int16)
                hot = jnp.where(places == row, one, nil)
                got = jnp.dot(xt_ref[...], hot, preferred_element_type=jnp.float32)
                weight = wide_ref[j]
                total = total + got * jnp.concatenate([weight] * (CHUNK // lanes), axis=1)
            acc_ref[...] = total
            first = t * points
            weights = [slim_ref[pl.ds(j * parts, parts), :] for j in range(PRODUCTS, fanout)]
            for p in range(points):
                total = None
                for j in range(PRODUCTS, fanout):
                    line = pl.multiple_of(near_ref[j, at + first + p], parts)
                    term = fine_ref[pl.ds(line, parts), :] * weights[j - PRODUCTS]
                    total = term if total is None else total + term
                sums_ref[pl.ds(pl.multiple_of((first + p) * parts, parts), parts), :] = total

        for i in range(parts):
            code_ref[pl.ds(at, CHUNK), i * lanes : (i + 1) * lanes] = (
                acc_ref[i * lanes : (i + 1) * lanes, :].T
                + sums_ref[pl.ds(i, CHUNK, stride=parts), :]
            ).astype(jnp.bfloat16)

    for b in range(in_blocks):
        here = pl.ds(pl.multiple_of(order_ref[b] * piece, piece), piece)
        features_ref[pl.ds(b * piece, piece), :] = x_ref[here, :]
        encoded_ref[pl.ds(b * piece, piece), :] = code_ref[here, :]


def attention_kernel(
    mode,
    owners,
    x_ref,
    code_ref,
    mixing_ref,
    gain_ref,
    qkv_ref,
    out_w_ref,
    out_ref,
    updated_ref,
    qt_ref,
    k_ref,
    vt_ref,
    mixed_ref,
    result_ref,
    *extra,
):
    rows, width = x_ref.shape
    lanes = 128
    chunks = rows // CHUNK
    if mode != "alone":
        me, mine = lax.axis_index("grp"), lax.axis_index("dev")
        landed_ref, turn_send, turn_recv = extra[:3]
        peers = [(me, around(owners, mine, k)) for k in range(1, owners)]
        if mode == "home":
            mate, over, _ = neighbours_of(4, owners)
            peers += [mate, over]
        entered = greet(peers)
    gain = gain_ref[...]
    scale = HEAD_DIM**-0.5 * math.log2(math.e)

    @pl.loop(0, chunks)
    def _(c):
        here = pl.ds(pl.multiple_of(c * CHUNK, CHUNK), CHUNK)

        updated = x_ref[here, :].astype(jnp.float32) + jnp.dot(
            code_ref[here, :], mixing_ref[...], preferred_element_type=jnp.float32
        )
        updated_ref[here, :] = updated
        centre = jnp.mean(updated, axis=-1, keepdims=True)
        moved = updated - centre
        spread = jnp.mean(moved * moved, axis=-1, keepdims=True)
        normed = (moved * lax.rsqrt(spread + EPSILON) * gain).astype(jnp.bfloat16)
        project = jnp.dot(normed, qkv_ref[...], preferred_element_type=jnp.float32)
        qt_ref[:, here] = (project[:, :width] * scale).T.astype(jnp.bfloat16)
        k_ref[here, :] = project[:, width : 2 * width].astype(jnp.bfloat16)
        values = project[:, 2 * width :].T.astype(jnp.bfloat16)
        for h in range(HEADS):
            vt_ref[h, :HEAD_DIM, here] = values[h * HEAD_DIM : (h + 1) * HEAD_DIM]

    vt_ref[:, HEAD_DIM:, :] = jnp.ones((HEADS, ONES, rows), jnp.bfloat16)

    if mode != "alone":
        share = rows // owners

        def outgoing(k):
            return pltpu.make_async_remote_copy(
                result_ref.at[pl.ds(pl.multiple_of(k * share, share), share)],
                landed_ref.at[pl.ds(pl.multiple_of(mine * share, share), share)],
                turn_send.at[k],
                turn_recv.at[k],
                device_id=(me, around(owners, mine, k + 1)),
                device_id_type=MESH,
            )

        def arriving(k):
            return pltpu.make_async_remote_copy(
                result_ref.at[pl.ds(pl.multiple_of(k * share, share), share)],
                landed_ref.at[
                    pl.ds(pl.multiple_of(around(owners, mine, -1 - k) * share, share), share)
                ],
                turn_send.at[k],
                turn_recv.at[k],
                device_id=(me, around(owners, mine, k + 1)),
                device_id_type=MESH,
            )

        entered()

    @pl.loop(0, chunks)
    def _(c):
        here = pl.ds(pl.multiple_of(c * CHUNK, CHUNK), CHUNK)

        def scored(h):
            pair = h // 2
            zero = jnp.zeros((HEAD_DIM, CHUNK), jnp.bfloat16)
            query = qt_ref[pl.ds(h * HEAD_DIM, HEAD_DIM), here]
            padded = jnp.concatenate([query, zero] if h % 2 == 0 else [zero, query], axis=0)
            return jnp.dot(
                k_ref[:, pair * lanes : (pair + 1) * lanes],
                padded,
                preferred_element_type=jnp.float32,
            )

        scores = scored(0)
        for h in range(HEADS):
            following = scored(h + 1) if h + 1 < HEADS else None
            peak = jnp.max(scores, axis=0, keepdims=True)
            powers = jnp.exp2(scores - peak).astype(jnp.bfloat16)
            mixed = jnp.dot(vt_ref[h], powers, preferred_element_type=jnp.float32)
            mixed_ref[pl.ds(h * HEAD_DIM, HEAD_DIM), :] = (
                mixed[:HEAD_DIM] / mixed[HEAD_DIM : HEAD_DIM + 1]
            )
            scores = following
        mixed = mixed_ref[...].T.astype(jnp.bfloat16)
        result_ref[here, :] = (
            updated_ref[here, :]
            + jnp.dot(mixed, out_w_ref[...], preferred_element_type=jnp.float32)
        ).astype(jnp.bfloat16)
        if mode != "alone":
            for i in range(CHUNK // share):
                k = c * (CHUNK // share) + i

                @pl.when(k < owners - 1)
                def _():
                    outgoing(k).start()

    if mode == "alone":
        out_ref[...] = result_ref[...]
        return
    landed_ref[pl.ds(pl.multiple_of(mine * share, share), share), :] = result_ref[
        pl.ds((owners - 1) * share, share), :
    ]
    if mode == "regroup":
        for k in range(owners - 1):
            arriving(k).wait_recv()
        out_ref[...] = landed_ref[...]
        for k in range(owners - 1):
            outgoing(k).wait_send()
        return

    over_send, over_recv, own_send, own_recv, far_send, far_recv = extra[3:]

    def onward(i, source, landing, send, recv, device):
        sender = mine if i == 0 else around(owners, mine, -i)
        at = pl.multiple_of(sender * share, share)
        return pltpu.make_async_remote_copy(
            landed_ref.at[pl.ds(source * rows + at, share)],
            landed_ref.at[pl.ds(landing * rows + at, share)],
            send.at[i],
            recv.at[i],
            device_id=device,
            device_id_type=MESH,
        )

    overs = [onward(i, 0, 1, over_send, over_recv, over) for i in range(owners)]
    owns = [onward(i, 0, 2, own_send, own_recv, mate) for i in range(owners)]
    fars = [onward(i, 1, 3, far_send, far_recv, mate) for i in range(owners)]
    for i in range(owners + 1):
        if i < owners:
            if i > 0:
                arriving(i - 1).wait_recv()
            overs[i].start()
            owns[i].start()
        if i > 0:
            overs[i - 1].wait_recv()
            fars[i - 1].start()
    for copy in owns + fars:
        copy.wait_recv()
    out_ref[...] = landed_ref[...]
    for copy in overs + owns + fars:
        copy.wait_send()
    for k in range(owners - 1):
        outgoing(k).wait_send()


def place_kernel(home_ref, source_ref, out_ref):
    pieces = home_ref.shape[0]
    piece = out_ref.shape[0] // pieces
    last = source_ref.shape[0] // piece
    for b in range(pieces):
        live = home_ref[b] < last
        here = pl.multiple_of(jnp.minimum(home_ref[b], last - 1) * piece, piece)
        found = source_ref[pl.ds(here, piece), :]
        out_ref[pl.ds(b * piece, piece), :] = jnp.where(live, found, jnp.zeros_like(found))


def put_home(source, home, piece):
    vmem = pl.BlockSpec(memory_space=pltpu.VMEM)
    return pl.pallas_call(
        place_kernel,
        out_shape=jax.ShapeDtypeStruct((home.shape[0] * piece, source.shape[1]), source.dtype),
        in_specs=[pl.BlockSpec(memory_space=pltpu.SMEM), vmem],
        out_specs=vmem,
        compiler_params=pltpu.CompilerParams(vmem_limit_bytes=LIMIT),
        name="put_home",
    )(home, source)


def run_block(source, lines, params, fetch, order, rows, mode="alone", owners=1):
    depth, mixing, gain, w_qkv, w_out = params
    width = source.shape[1]
    fanout = lines.shape[0]
    parts = width // 128
    vmem = pl.BlockSpec(memory_space=pltpu.VMEM)
    smem = pl.BlockSpec(memory_space=pltpu.SMEM)
    patch = jax.ShapeDtypeStruct((rows, width), jnp.bfloat16)
    features, encoded = pl.pallas_call(
        encode_kernel,
        out_shape=(patch, patch),
        in_specs=[smem] * 3 + [vmem] * 4,
        out_specs=(vmem, vmem),
        scratch_shapes=[
            pltpu.VMEM((rows, width), jnp.bfloat16),
            pltpu.VMEM((width, rows), jnp.bfloat16),
            pltpu.VMEM((rows * parts, 128), jnp.float32),
            pltpu.VMEM((fanout * parts, 128), jnp.float32),
            pltpu.VMEM((CHUNK * parts, 128), jnp.float32),
            pltpu.VMEM((PRODUCTS, width, 128), jnp.float32),
            pltpu.VMEM((width, CHUNK), jnp.float32),
            pltpu.VMEM((rows, width), jnp.bfloat16),
        ],
        compiler_params=pltpu.CompilerParams(vmem_limit_bytes=LIMIT),
        cost_estimate=pl.CostEstimate(
            flops=2 * fanout * rows * rows * width, bytes_accessed=4 << 20, transcendentals=0
        ),
        name="encode",
    )(fetch, order, lines, source, lines, depth, depth.T)
    extra = []
    settings = pltpu.CompilerParams(vmem_limit_bytes=LIMIT)
    copies = 4 if mode == "home" else 1
    if mode != "alone":
        extra = [
            pltpu.VMEM((copies * rows, width), jnp.bfloat16),
            pltpu.SemaphoreType.DMA((owners - 1,)),
            pltpu.SemaphoreType.DMA((owners - 1,)),
        ]
        settings = pltpu.CompilerParams(
            vmem_limit_bytes=LIMIT,
            collective_id=1 if mode == "regroup" else 2,
            has_side_effects=True,
        )
    if mode == "home":
        extra += [pltpu.SemaphoreType.DMA((owners,))] * 6
    return pl.pallas_call(
        functools.partial(attention_kernel, mode, owners),
        out_shape=jax.ShapeDtypeStruct((copies * rows, width), jnp.bfloat16),
        in_specs=[vmem] * 6,
        out_specs=vmem,
        scratch_shapes=[
            pltpu.VMEM((rows, width), jnp.float32),
            pltpu.VMEM((width, rows), jnp.bfloat16),
            pltpu.VMEM((rows, width), jnp.bfloat16),
            pltpu.VMEM((HEADS, HEAD_DIM + ONES, rows), jnp.bfloat16),
            pltpu.VMEM((width, CHUNK), jnp.float32),
            pltpu.VMEM((rows, width), jnp.bfloat16),
        ]
        + extra,
        compiler_params=settings,
        cost_estimate=pl.CostEstimate(
            flops=10 * rows * width * width, bytes_accessed=8 << 20, transcendentals=8 << 20
        ),
        name="attention_" + mode,
    )(features, encoded, mixing, gain.reshape(1, width), w_qkv, w_out)


def body(
    home_points,
    counts,
    owner_group,
    neighbors_home,
    hilbert_target,
    neighbors_second,
    depth_first,
    mixing_first,
    gain_first,
    w_qkv_first,
    w_out_first,
    depth_second,
    mixing_second,
    gain_second,
    w_qkv_second,
    w_out_second,
):
    groups = lax.axis_size("grp")
    owners = lax.axis_size("dev")
    chips = groups // CORES
    me = lax.axis_index("grp")
    place_x, core = me // CORES, me % CORES
    mine = lax.axis_index("dev")
    home_rows, width = home_points.shape
    slot_count = owner_group.shape[0]
    rows = home_rows // slot_count
    block_count = hilbert_target.shape[0]
    piece = rows // block_count
    fanout = neighbors_home.shape[0]
    mate = [(i, i ^ 1) for i in range(groups)]
    first_params = (depth_first, mixing_first, gain_first, w_qkv_first, w_out_first)
    second_params = (depth_second, mixing_second, gain_second, w_qkv_second, w_out_second)

    if chips == 2 and slot_count == 2 and owners * CAPACITY == block_count:
        filled = jnp.arange(slot_count) < counts[0]
        wanted = jnp.where(filled, owner_group, -1)
        meta = jnp.concatenate(
            [
                jnp.broadcast_to(wanted[:, None], (slot_count, width)),
                jnp.broadcast_to(
                    jnp.pad(hilbert_target, (0, width - block_count))[None], (6, width)
                ),
            ]
        ).astype(jnp.int32)
        points, lines, metas = to_owners(home_points, neighbors_home, meta, owners)
        counter = jnp.arange(block_count)

        def slot_places(table):
            aim = table // block_count
            same = aim[:, :, None] == aim[:, None, :]
            rank = jnp.sum(same & (counter[:, None] > counter[None, :]), axis=2)
            return aim, rank

        told = metas[:, slot_count, :block_count]
        aim, rank = slot_places(told)
        turn = ((aim[3] - mine - 1) % owners) * CAPACITY + rank[3]
        order = jnp.sum(
            jnp.where(turn[None, :] == counter[:, None], counter[None, :], 0), axis=1
        ).astype(jnp.int32)
        straight = jnp.arange(block_count, dtype=jnp.int32)
        incoming = run_block(
            points, lines, first_params, straight, order, rows, "regroup", owners
        )
        sender = (mine - jnp.arange(owners)) % owners
        sent_at = (sender[:, None] * CAPACITY + rank[3:]).reshape(-1)
        goal = mine * block_count + counter
        fetch = jnp.sum(
            jnp.where(told[3:].reshape(-1)[None, :] == goal[:, None], sent_at[None, :], 0), axis=1
        ).astype(jnp.int32)
        wheel = (counter + (mine + 1) * CAPACITY) % block_count
        back = jnp.sum(
            jnp.where(fetch[None, :] == wheel[:, None], counter[None, :], 0), axis=1
        ).astype(jnp.int32)
        places = aim * CAPACITY + rank
        places = jnp.stack([places[3], places[1], places[0], places[2]])
        buffer = (owner_group // CORES != place_x) + 2 * (owner_group % CORES != core)
        home = jnp.where(
            filled[:, None], buffer[:, None] * block_count + places[buffer], 4 * block_count
        )
        buffers = run_block(
            incoming,
            neighbors_second * (width // 128),
            second_params,
            fetch,
            back,
            rows,
            "home",
            owners,
        )
        return put_home(buffers, home.reshape(-1).astype(jnp.int32), piece)

    targets = lax.all_gather(hilbert_target, "dev", axis=0, tiled=True).reshape(
        owners, block_count
    )

    filled = jnp.arange(slot_count) < counts[0]
    wanted = jnp.where(filled, owner_group, -1)
    tiles = home_points.reshape(slot_count, rows, width)
    lists = jnp.transpose(neighbors_home.reshape(fanout, slot_count, rows), (1, 0, 2))
    stamped = jnp.concatenate(
        [lists, jnp.broadcast_to(wanted[:, None, None], (slot_count, 1, rows))], axis=1
    )
    other_tiles = lax.ppermute(tiles, "grp", mate)
    other_stamped = lax.ppermute(stamped, "grp", mate)
    other_wanted = other_stamped[:, fanout, 0]

    def candidate(target):
        here, there = wanted == target, other_wanted == target
        at_here = jnp.sum(jnp.where(here, jnp.arange(slot_count), 0))
        at_there = jnp.sum(jnp.where(there, jnp.arange(slot_count), 0))
        ours = jnp.any(here)
        pick = lambda a, b: jnp.where(
            ours,
            lax.dynamic_index_in_dim(a, at_here, 0, keepdims=False),
            lax.dynamic_index_in_dim(b, at_there, 0, keepdims=False),
        )
        return ours | jnp.any(there), pick(tiles, other_tiles), pick(stamped, other_stamped)

    held, points, stamps = candidate(me)
    for r in range(1, chips):
        target = ((place_x + r) % chips) * CORES + core
        _, points_out, stamps_out = candidate(target)
        over = [
            (x * CORES + c, ((x + r) % chips) * CORES + c)
            for x in range(chips)
            for c in range(CORES)
        ]
        points_in = lax.ppermute(points_out, "grp", over)
        stamps_in = lax.ppermute(stamps_out, "grp", over)
        take = stamps_in[fanout, 0] == me
        points = jnp.where(take, points_in, points)
        stamps = jnp.where(take, stamps_in, stamps)

    slots = owners * CAPACITY
    counter = jnp.arange(block_count)
    destination = targets // block_count
    same = destination[:, :, None] == destination[:, None, :]
    rank = jnp.sum(same & (counter[:, None] > counter[None, :]), axis=2)
    places = destination * CAPACITY + rank
    place = lax.dynamic_index_in_dim(places, mine, 0, keepdims=False)
    order = jnp.sum(
        jnp.where(place[None, :] == jnp.arange(slots)[:, None], counter[None, :], 0), axis=1
    ).astype(jnp.int32)
    sent_at = (jnp.arange(owners)[:, None] * CAPACITY + rank).reshape(-1)
    flat = targets.reshape(-1)
    goal = mine * block_count + counter
    fetch = jnp.sum(
        jnp.where(flat[None, :] == goal[:, None], sent_at[None, :], 0), axis=1
    ).astype(jnp.int32)
    back = jnp.sum(
        jnp.where(fetch[None, :] == jnp.arange(slots)[:, None], counter[None, :], 0), axis=1
    ).astype(jnp.int32)

    straight = jnp.arange(block_count, dtype=jnp.int32)
    section_one = run_block(
        points, stamps[:fanout] * (width // 128), first_params, straight, straight, rows
    )
    outgoing = section_one.reshape(block_count, piece, width)[order].reshape(-1, width)
    swap = lambda a: lax.all_to_all(a, "dev", split_axis=0, concat_axis=0, tiled=True)
    incoming = swap(outgoing)
    section_two = run_block(
        incoming, neighbors_second * (width // 128), second_params, fetch, straight, rows
    )
    backward = section_two.reshape(block_count, piece, width)[back].reshape(-1, width)
    returned = swap(backward).reshape(slots, piece, width)
    finished = returned[place].reshape(rows, width)

    gathered = [finished]
    for r in range(1, chips):
        over = [
            (x * CORES + c, ((x + r) % chips) * CORES + c)
            for x in range(chips)
            for c in range(CORES)
        ]
        gathered.append(lax.ppermute(finished, "grp", over))
    stack = jnp.stack(gathered)
    other = lax.ppermute(stack, "grp", mate)
    shift = (place_x - owner_group // CORES) % chips
    ours = owner_group % CORES == core
    parts = [
        jnp.where(
            filled[s],
            jnp.where(
                ours[s],
                lax.dynamic_index_in_dim(stack, shift[s], 0, keepdims=False),
                lax.dynamic_index_in_dim(other, shift[s], 0, keepdims=False),
            ),
            jnp.zeros((), jnp.bfloat16),
        )
        for s in range(slot_count)
    ]
    return jnp.concatenate(parts, axis=0)


def solution(mesh):
    return jax.shard_map(
        body,
        mesh=mesh,
        in_specs=(
            P(("grp", "dev"), None),
            P(("grp", "dev")),
            P(("grp", "dev")),
            P(None, ("grp", "dev")),
            P(("grp", "dev")),
            P(None, ("grp", "dev")),
            P(),
            P(),
            P(),
            P(),
            P(),
            P(),
            P(),
            P(),
            P(),
            P(),
        ),
        out_specs=P(("grp", "dev"), None),
        check_vma=False,
    )
```

```python
import functools
import math

import jax
import jax.numpy as jnp
from jax import lax
from jax.experimental import pallas as pl
from jax.experimental.pallas import tpu as pltpu
from jax.sharding import PartitionSpec as P

HEADS = 8
HEAD_DIM = 64
CAPACITY = 2
CORES = 2
CHUNK = 256
EPSILON = 1e-05
ONES = 16
TURNS = 4
QUARTERS = 4
LIMIT = 56 * 1024 * 1024


MESH = pl.DeviceIdType.MESH


def around(size, at, step):
    return lax.rem(at + step + size, size)


def greet(peers):
    barrier = pltpu.get_barrier_semaphore()
    for peer in peers:
        pl.semaphore_signal(barrier, inc=1, device_id=peer, device_id_type=MESH)
    return lambda: pl.semaphore_wait(barrier, len(peers))


def neighbours_of(groups, owners):
    me, mine = lax.axis_index("grp"), lax.axis_index("dev")
    chip, core = me // CORES, lax.rem(me, CORES)
    mate = (chip * CORES + 1 - core, mine)
    over = ((1 - chip) * CORES + core, mine)
    slant = ((1 - chip) * CORES + 1 - core, mine)
    return mate, over, slant


def owners_kernel(
    owners,
    points_ref,
    lists_ref,
    meta_ref,
    points_out,
    lists_out,
    metas_out,
    give_points,
    give_lists,
    mate_points,
    mate_lists,
    out_points,
    out_lists,
    in_points,
    in_lists,
    metas_ref,
    meta_send,
    meta_recv,
    mate_send,
    mate_recv,
    over_send,
    over_recv,
):
    me, mine = lax.axis_index("grp"), lax.axis_index("dev")
    rows = points_out.shape[0]
    part = rows // QUARTERS
    mate, over, slant = neighbours_of(4, owners)
    peers = [mate, over, slant] + [(me, around(owners, mine, k)) for k in range(1, owners)]
    entered = greet(peers)

    def flags(target):
        return [meta_ref[slot : slot + 1, :] == target for slot in range(2)]

    def chosen_points(target, q):
        one, two = [jnp.where(f, 1.0, 0.0).astype(jnp.bfloat16) for f in flags(target)]
        return (
            points_ref[pl.ds(q * part, part), :] * one
            + points_ref[pl.ds(rows + q * part, part), :] * two
        )

    def chosen_lists(target):
        one, two = [
            jnp.concatenate([jnp.where(f, 1, 0)] * (rows // f.shape[1]), axis=1)
            for f in flags(target)
        ]
        return lists_ref[:, :rows] * one + lists_ref[:, rows:] * two

    def copy(source, landing, send, recv, i, device):
        return pltpu.make_async_remote_copy(
            source, landing, send.at[i], recv.at[i], device_id=device, device_id_type=MESH
        )

    metas = [
        copy(meta_ref, metas_ref.at[i if i < 3 else i + 1], meta_send, meta_recv, i, peer)
        for i, peer in enumerate(peers)
    ]
    spans = [pl.ds(q * part, part) for q in range(QUARTERS)]
    gives = [
        [
            copy(
                give_points.at[half, span],
                mate_points.at[half, span],
                mate_send,
                mate_recv,
                half * QUARTERS + q,
                mate,
            )
            for q, span in enumerate(spans)
        ]
        + [
            copy(
                give_lists.at[half],
                mate_lists.at[half],
                mate_send,
                mate_recv,
                2 * QUARTERS + half,
                mate,
            )
        ]
        for half in range(2)
    ]
    sends = [
        copy(out_points.at[span], in_points.at[span], over_send, over_recv, q, over)
        for q, span in enumerate(spans)
    ] + [copy(out_lists, in_lists, over_send, over_recv, QUARTERS, over)]

    entered()
    for q, span in enumerate(spans):
        give_points[0, span] = chosen_points(slant[0], q)
        gives[0][q].start()
    give_lists[0] = chosen_lists(slant[0])
    gives[0][QUARTERS].start()
    for move in metas:
        move.start()
    metas_ref[3] = meta_ref[...]
    for q, span in enumerate(spans):
        kept = chosen_points(over[0], q)
        gives[0][q].wait_recv()
        out_points[span, :] = kept + mate_points[0, span]
        sends[q].start()
    kept = chosen_lists(over[0])
    gives[0][QUARTERS].wait_recv()
    out_lists[...] = kept + mate_lists[0]
    sends[QUARTERS].start()
    for q, span in enumerate(spans):
        give_points[1, span] = chosen_points(mate[0], q)
        gives[1][q].start()
    give_lists[1] = chosen_lists(mate[0])
    gives[1][QUARTERS].start()
    for q, span in enumerate(spans):
        kept = chosen_points(me, q)
        gives[1][q].wait_recv()
        points_out[span, :] = kept + mate_points[1, span]
    kept = chosen_lists(me)
    gives[1][QUARTERS].wait_recv()
    kept = kept + mate_lists[1]
    for move in metas:
        move.wait_recv()
    metas_out[...] = metas_ref[...]
    for q, span in enumerate(spans):
        sends[q].wait_recv()
        points_out[span, :] = points_out[span, :] + in_points[span, :]
    sends[QUARTERS].wait_recv()
    lists_out[...] = (kept + in_lists[...]) * (points_ref.shape[1] // 128)
    for move in metas + gives[0] + gives[1] + sends:
        move.wait_send()


def to_owners(points, lists, meta, owners):
    rows, width = points.shape[0] // 2, points.shape[1]
    fanout = lists.shape[0]
    vmem = pl.BlockSpec(memory_space=pltpu.VMEM)
    count = owners + 2
    return pl.pallas_call(
        functools.partial(owners_kernel, owners),
        out_shape=(
            jax.ShapeDtypeStruct((rows, width), points.dtype),
            jax.ShapeDtypeStruct((fanout, rows), jnp.int32),
            jax.ShapeDtypeStruct((count + 1,) + meta.shape, jnp.int32),
        ),
        in_specs=[vmem] * 3,
        out_specs=(vmem,) * 3,
        scratch_shapes=[
            pltpu.VMEM((2, rows, width), points.dtype),
            pltpu.VMEM((2, fanout, rows), jnp.int32),
            pltpu.VMEM((2, rows, width), points.dtype),
            pltpu.VMEM((2, fanout, rows), jnp.int32),
            pltpu.VMEM((rows, width), points.dtype),
            pltpu.VMEM((fanout, rows), jnp.int32),
            pltpu.VMEM((rows, width), points.dtype),
            pltpu.VMEM((fanout, rows), jnp.int32),
            pltpu.VMEM((count + 1,) + meta.shape, jnp.int32),
            pltpu.SemaphoreType.DMA((count,)),
            pltpu.SemaphoreType.DMA((count,)),
            pltpu.SemaphoreType.DMA((2 * QUARTERS + 2,)),
            pltpu.SemaphoreType.DMA((2 * QUARTERS + 2,)),
            pltpu.SemaphoreType.DMA((QUARTERS + 1,)),
            pltpu.SemaphoreType.DMA((QUARTERS + 1,)),
        ],
        compiler_params=pltpu.CompilerParams(
            collective_id=0, has_side_effects=True, vmem_limit_bytes=56 * 1024 * 1024
        ),
        cost_estimate=pl.CostEstimate(flops=1 << 20, bytes_accessed=8 << 20, transcendentals=0),
        name="to_owners",
    )(points, lists, meta)


def encode_kernel(
    products,
    fetch_ref,
    order_ref,
    near_ref,
    source_ref,
    lists_ref,
    depth_ref,
    turned_ref,
    features_ref,
    encoded_ref,
    x_ref,
    xt_ref,
    fine_ref,
    slim_ref,
    sums_ref,
    wide_ref,
    acc_ref,
    code_ref,
):
    rows, width = x_ref.shape
    fanout = depth_ref.shape[0]
    in_blocks = fetch_ref.shape[0]
    piece = rows // in_blocks
    chunks = rows // CHUNK
    lanes = 128
    parts = width // lanes
    for b in range(in_blocks):
        x_ref[pl.ds(b * piece, piece), :] = source_ref[
            pl.ds(pl.multiple_of(fetch_ref[b] * piece, piece), piece), :
        ]
    xt_ref[...] = x_ref[...].T
    for c in range(parts):
        fine_ref[pl.ds(c, rows, stride=parts), :] = x_ref[:, c * lanes : (c + 1) * lanes].astype(
            jnp.float32
        )
        slim_ref[pl.ds(c, fanout, stride=parts), :] = depth_ref[:, c * lanes : (c + 1) * lanes]
    for j in range(products):
        wide_ref[j] = jnp.broadcast_to(turned_ref[:, j : j + 1], (width, lanes))
    places = (lax.broadcasted_iota(jnp.int32, (rows, CHUNK), 0) * parts).astype(jnp.int16)
    one, nil = jnp.bfloat16(1), jnp.bfloat16(0)
    step = products // TURNS
    points = CHUNK // TURNS

    @pl.loop(0, chunks)
    def _(c):
        at = pl.multiple_of(c * CHUNK, CHUNK)
        acc_ref[...] = jnp.zeros_like(acc_ref)

        @pl.loop(0, TURNS)
        def _(t):
            total = acc_ref[...]
            for dj in range(step):
                j = t * step + dj
                row = lists_ref[pl.ds(j, 1), pl.ds(at, CHUNK)].astype(jnp.int16)
                hot = jnp.where(places == row, one, nil)
                got = jnp.dot(xt_ref[...], hot, preferred_element_type=jnp.float32)
                weight = wide_ref[j]
                total = total + got * jnp.concatenate([weight] * (CHUNK // lanes), axis=1)
            acc_ref[...] = total
            first = t * points
            base = (c * TURNS + t) * (fanout * points)
            weights = [slim_ref[pl.ds(j * parts, parts), :] for j in range(products, fanout)]
            for p in range(points):
                total = None
                for j in range(products, fanout):
                    line = pl.multiple_of(near_ref[base + (j * points + p)], parts)
                    term = fine_ref[pl.ds(line, parts), :] * weights[j - products]
                    total = term if total is None else total + term
                sums_ref[pl.ds(pl.multiple_of((first + p) * parts, parts), parts), :] = total

        for i in range(parts):
            code_ref[pl.ds(at, CHUNK), i * lanes : (i + 1) * lanes] = (
                acc_ref[i * lanes : (i + 1) * lanes, :].T
                + sums_ref[pl.ds(i, CHUNK, stride=parts), :]
            ).astype(jnp.bfloat16)

    for b in range(in_blocks):
        here = pl.ds(pl.multiple_of(order_ref[b] * piece, piece), piece)
        features_ref[pl.ds(b * piece, piece), :] = x_ref[here, :]
        encoded_ref[pl.ds(b * piece, piece), :] = code_ref[here, :]


def attention_kernel(
    mode,
    owners,
    x_ref,
    code_ref,
    mixing_ref,
    gain_ref,
    qkv_ref,
    out_w_ref,
    out_ref,
    updated_ref,
    qt_ref,
    k_ref,
    vt_ref,
    mixed_ref,
    result_ref,
    *extra,
):
    rows, width = x_ref.shape
    lanes = 128
    chunks = rows // CHUNK
    if mode != "alone":
        me, mine = lax.axis_index("grp"), lax.axis_index("dev")
        landed_ref, turn_send, turn_recv = extra[:3]
        peers = [(me, around(owners, mine, k)) for k in range(1, owners)]
        if mode == "home":
            mate, over, _ = neighbours_of(4, owners)
            peers += [mate, over]
        entered = greet(peers)
    gain = gain_ref[...]
    scale = HEAD_DIM**-0.5 * math.log2(math.e)

    @pl.loop(0, chunks)
    def _(c):
        here = pl.ds(pl.multiple_of(c * CHUNK, CHUNK), CHUNK)

        updated = x_ref[here, :].astype(jnp.float32) + jnp.dot(
            code_ref[here, :], mixing_ref[...], preferred_element_type=jnp.float32
        )
        updated_ref[here, :] = updated
        centre = jnp.mean(updated, axis=-1, keepdims=True)
        moved = updated - centre
        spread = jnp.mean(moved * moved, axis=-1, keepdims=True)
        normed = (moved * lax.rsqrt(spread + EPSILON) * gain).astype(jnp.bfloat16)
        project = jnp.dot(normed, qkv_ref[...], preferred_element_type=jnp.float32)
        qt_ref[:, here] = (project[:, :width] * scale).T.astype(jnp.bfloat16)
        k_ref[here, :] = project[:, width : 2 * width].astype(jnp.bfloat16)
        values = project[:, 2 * width :].T.astype(jnp.bfloat16)
        for h in range(HEADS):
            vt_ref[h, :HEAD_DIM, here] = values[h * HEAD_DIM : (h + 1) * HEAD_DIM]

    vt_ref[:, HEAD_DIM:, :] = jnp.ones((HEADS, ONES, rows), jnp.bfloat16)

    if mode != "alone":
        share = rows // owners

        def outgoing(k):
            return pltpu.make_async_remote_copy(
                result_ref.at[pl.ds(pl.multiple_of(k * share, share), share)],
                landed_ref.at[pl.ds(pl.multiple_of(mine * share, share), share)],
                turn_send.at[k],
                turn_recv.at[k],
                device_id=(me, around(owners, mine, k)),
                device_id_type=MESH,
            )

        def arriving(k):
            return pltpu.make_async_remote_copy(
                result_ref.at[pl.ds(pl.multiple_of(k * share, share), share)],
                landed_ref.at[
                    pl.ds(pl.multiple_of(around(owners, mine, -k) * share, share), share)
                ],
                turn_send.at[k],
                turn_recv.at[k],
                device_id=(me, around(owners, mine, k)),
                device_id_type=MESH,
            )

        if mode == "home":
            over_send, over_recv, own_send, own_recv, far_send, far_recv = extra[3:]

        def onward(k, source, landing, send, recv, device):
            at = pl.multiple_of(around(owners, mine, -k) * share, share)
            return pltpu.make_async_remote_copy(
                landed_ref.at[pl.ds(source * rows + at, share)],
                landed_ref.at[pl.ds(landing * rows + at, share)],
                send.at[k],
                recv.at[k],
                device_id=device,
                device_id_type=MESH,
            )

        def to_over(k):
            return onward(k, 0, 1, over_send, over_recv, over)

        def to_mate(k):
            return onward(k, 0, 2, own_send, own_recv, mate)

        def far_to_mate(k):
            return onward(k, 1, 3, far_send, far_recv, mate)

        def forward(k):
            arriving(k).wait_recv()
            to_over(k).start()
            to_mate(k).start()

        each = CHUNK // share
        entered()

    @pl.loop(0, chunks)
    def _(c):
        here = pl.ds(pl.multiple_of(c * CHUNK, CHUNK), CHUNK)

        def scored(h):
            pair = h // 2
            zero = jnp.zeros((HEAD_DIM, CHUNK), jnp.bfloat16)
            query = qt_ref[pl.ds(h * HEAD_DIM, HEAD_DIM), here]
            padded = jnp.concatenate([query, zero] if h % 2 == 0 else [zero, query], axis=0)
            return jnp.dot(
                k_ref[:, pair * lanes : (pair + 1) * lanes],
                padded,
                preferred_element_type=jnp.float32,
            )

        scores = scored(0)
        for h in range(HEADS):
            following = scored(h + 1) if h + 1 < HEADS else None
            peak = jnp.max(scores, axis=0, keepdims=True)
            powers = jnp.exp2(scores - peak).astype(jnp.bfloat16)
            mixed = jnp.dot(vt_ref[h], powers, preferred_element_type=jnp.float32)
            mixed_ref[pl.ds(h * HEAD_DIM, HEAD_DIM), :] = (
                mixed[:HEAD_DIM] / mixed[HEAD_DIM : HEAD_DIM + 1]
            )
            scores = following
        mixed = mixed_ref[...].T.astype(jnp.bfloat16)
        result_ref[here, :] = (
            updated_ref[here, :]
            + jnp.dot(mixed, out_w_ref[...], preferred_element_type=jnp.float32)
        ).astype(jnp.bfloat16)
        if mode == "alone":
            return

        @pl.when(c == 0)
        def _():
            landed_ref[pl.ds(pl.multiple_of(mine * share, share), share), :] = result_ref[
                pl.ds(0, share), :
            ]
            for k in range(1, each):
                outgoing(k).start()
            if mode == "home":
                to_over(0).start()
                to_mate(0).start()

        @pl.when(c > 0)
        def _():
            for i in range(each):
                outgoing(c * each + i).start()

        if mode == "home":

            @pl.when(c == 1)
            def _():
                for k in range(1, each):
                    forward(k)

            @pl.when(c > 1)
            def _():
                for i in range(each):
                    forward((c - 1) * each + i)

    if mode == "alone":
        out_ref[...] = result_ref[...]
        return
    if mode == "regroup":
        for k in range(1, owners):
            arriving(k).wait_recv()
        out_ref[...] = landed_ref[...]
        for k in range(1, owners):
            outgoing(k).wait_send()
        return

    done = 0
    for k in range(owners - each, owners):
        while done < k - 2:
            to_over(done).wait_recv()
            far_to_mate(done).start()
            done += 1
        forward(k)
    for k in range(done, owners):
        to_over(k).wait_recv()
        far_to_mate(k).start()
    for k in range(owners):
        to_mate(k).wait_recv()
        far_to_mate(k).wait_recv()
    out_ref[...] = landed_ref[...]
    for k in range(owners):
        to_over(k).wait_send()
        to_mate(k).wait_send()
        far_to_mate(k).wait_send()
    for k in range(1, owners):
        outgoing(k).wait_send()


def place_kernel(home_ref, source_ref, out_ref):
    pieces = home_ref.shape[0]
    piece = out_ref.shape[0] // pieces
    last = source_ref.shape[0] // piece
    for b in range(pieces):
        live = home_ref[b] < last
        here = pl.multiple_of(jnp.minimum(home_ref[b], last - 1) * piece, piece)
        found = source_ref[pl.ds(here, piece), :]
        out_ref[pl.ds(b * piece, piece), :] = jnp.where(live, found, jnp.zeros_like(found))


def put_home(source, home, piece):
    vmem = pl.BlockSpec(memory_space=pltpu.VMEM)
    return pl.pallas_call(
        place_kernel,
        out_shape=jax.ShapeDtypeStruct((home.shape[0] * piece, source.shape[1]), source.dtype),
        in_specs=[pl.BlockSpec(memory_space=pltpu.SMEM), vmem],
        out_specs=vmem,
        compiler_params=pltpu.CompilerParams(vmem_limit_bytes=LIMIT),
        name="put_home",
    )(home, source)


def run_block(source, lines, params, fetch, order, rows, products, mode="alone", owners=1):
    depth, mixing, gain, w_qkv, w_out = params
    width = source.shape[1]
    fanout = lines.shape[0]
    parts = width // 128
    vmem = pl.BlockSpec(memory_space=pltpu.VMEM)
    smem = pl.BlockSpec(memory_space=pltpu.SMEM)
    patch = jax.ShapeDtypeStruct((rows, width), jnp.bfloat16)
    near = lines.reshape(fanout, -1, CHUNK // TURNS).transpose(1, 0, 2).reshape(-1)
    features, encoded = pl.pallas_call(
        functools.partial(encode_kernel, products),
        out_shape=(patch, patch),
        in_specs=[smem] * 3 + [vmem] * 4,
        out_specs=(vmem, vmem),
        scratch_shapes=[
            pltpu.VMEM((rows, width), jnp.bfloat16),
            pltpu.VMEM((width, rows), jnp.bfloat16),
            pltpu.VMEM((rows * parts, 128), jnp.float32),
            pltpu.VMEM((fanout * parts, 128), jnp.float32),
            pltpu.VMEM((CHUNK * parts, 128), jnp.float32),
            pltpu.VMEM((products, width, 128), jnp.float32),
            pltpu.VMEM((width, CHUNK), jnp.float32),
            pltpu.VMEM((rows, width), jnp.bfloat16),
        ],
        compiler_params=pltpu.CompilerParams(vmem_limit_bytes=LIMIT),
        cost_estimate=pl.CostEstimate(
            flops=2 * fanout * rows * rows * width, bytes_accessed=4 << 20, transcendentals=0
        ),
        name="encode",
    )(fetch, order, near, source, lines, depth, depth.T)
    extra = []
    settings = pltpu.CompilerParams(vmem_limit_bytes=LIMIT)
    copies = 4 if mode == "home" else 1
    if mode != "alone":
        extra = [
            pltpu.VMEM((copies * rows, width), jnp.bfloat16),
            pltpu.SemaphoreType.DMA((owners,)),
            pltpu.SemaphoreType.DMA((owners,)),
        ]
        settings = pltpu.CompilerParams(
            vmem_limit_bytes=LIMIT,
            collective_id=1 if mode == "regroup" else 2,
            has_side_effects=True,
        )
    if mode == "home":
        extra += [pltpu.SemaphoreType.DMA((owners,))] * 6
    return pl.pallas_call(
        functools.partial(attention_kernel, mode, owners),
        out_shape=jax.ShapeDtypeStruct((copies * rows, width), jnp.bfloat16),
        in_specs=[vmem] * 6,
        out_specs=vmem,
        scratch_shapes=[
            pltpu.VMEM((rows, width), jnp.float32),
            pltpu.VMEM((width, rows), jnp.bfloat16),
            pltpu.VMEM((rows, width), jnp.bfloat16),
            pltpu.VMEM((HEADS, HEAD_DIM + ONES, rows), jnp.bfloat16),
            pltpu.VMEM((width, CHUNK), jnp.float32),
            pltpu.VMEM((rows, width), jnp.bfloat16),
        ]
        + extra,
        compiler_params=settings,
        cost_estimate=pl.CostEstimate(
            flops=10 * rows * width * width, bytes_accessed=8 << 20, transcendentals=8 << 20
        ),
        name="attention_" + mode,
    )(features, encoded, mixing, gain.reshape(1, width), w_qkv, w_out)


def body(
    home_points,
    counts,
    owner_group,
    neighbors_home,
    hilbert_target,
    neighbors_second,
    depth_first,
    mixing_first,
    gain_first,
    w_qkv_first,
    w_out_first,
    depth_second,
    mixing_second,
    gain_second,
    w_qkv_second,
    w_out_second,
):
    groups = lax.axis_size("grp")
    owners = lax.axis_size("dev")
    chips = groups // CORES
    me = lax.axis_index("grp")
    place_x, core = me // CORES, me % CORES
    mine = lax.axis_index("dev")
    home_rows, width = home_points.shape
    slot_count = owner_group.shape[0]
    rows = home_rows // slot_count
    block_count = hilbert_target.shape[0]
    piece = rows // block_count
    fanout = neighbors_home.shape[0]
    mate = [(i, i ^ 1) for i in range(groups)]
    first_params = (depth_first, mixing_first, gain_first, w_qkv_first, w_out_first)
    second_params = (depth_second, mixing_second, gain_second, w_qkv_second, w_out_second)

    if chips == 2 and slot_count == 2 and owners * CAPACITY == block_count:
        filled = jnp.arange(slot_count) < counts[0]
        wanted = jnp.where(filled, owner_group, -1)
        meta = jnp.concatenate(
            [
                jnp.broadcast_to(wanted[:, None], (slot_count, width)),
                jnp.broadcast_to(
                    jnp.pad(hilbert_target, (0, width - block_count))[None], (6, width)
                ),
            ]
        ).astype(jnp.int32)
        points, lines, metas = to_owners(home_points, neighbors_home, meta, owners)
        counter = jnp.arange(block_count)

        def slot_places(table):
            aim = table // block_count
            same = aim[:, :, None] == aim[:, None, :]
            rank = jnp.sum(same & (counter[:, None] > counter[None, :]), axis=2)
            return aim, rank

        told = metas[:, slot_count, :block_count]
        aim, rank = slot_places(told)
        own_aim, own_rank = slot_places(hilbert_target[None])
        turn = ((own_aim[0] - mine) % owners) * CAPACITY + own_rank[0]
        order = jnp.sum(
            jnp.where(turn[None, :] == counter[:, None], counter[None, :], 0), axis=1
        ).astype(jnp.int32)
        straight = jnp.arange(block_count, dtype=jnp.int32)
        incoming = run_block(
            points, lines, first_params, straight, order, rows, 16, "regroup", owners
        )
        sender = (mine - jnp.arange(owners)) % owners
        sent_at = (sender[:, None] * CAPACITY + rank[3:]).reshape(-1)
        goal = mine * block_count + counter
        fetch = jnp.sum(
            jnp.where(told[3:].reshape(-1)[None, :] == goal[:, None], sent_at[None, :], 0), axis=1
        ).astype(jnp.int32)
        wheel = (counter + mine * CAPACITY) % block_count
        back = jnp.sum(
            jnp.where(fetch[None, :] == wheel[:, None], counter[None, :], 0), axis=1
        ).astype(jnp.int32)
        places = aim * CAPACITY + rank
        places = jnp.stack([places[3], places[1], places[0], places[2]])
        buffer = (owner_group // CORES != place_x) + 2 * (owner_group % CORES != core)
        home = jnp.where(
            filled[:, None], buffer[:, None] * block_count + places[buffer], 4 * block_count
        )
        buffers = run_block(
            incoming,
            neighbors_second * (width // 128),
            second_params,
            fetch,
            back,
            rows,
            20,
            "home",
            owners,
        )
        return put_home(buffers, home.reshape(-1).astype(jnp.int32), piece)

    targets = lax.all_gather(hilbert_target, "dev", axis=0, tiled=True).reshape(
        owners, block_count
    )

    filled = jnp.arange(slot_count) < counts[0]
    wanted = jnp.where(filled, owner_group, -1)
    tiles = home_points.reshape(slot_count, rows, width)
    lists = jnp.transpose(neighbors_home.reshape(fanout, slot_count, rows), (1, 0, 2))
    stamped = jnp.concatenate(
        [lists, jnp.broadcast_to(wanted[:, None, None], (slot_count, 1, rows))], axis=1
    )
    other_tiles = lax.ppermute(tiles, "grp", mate)
    other_stamped = lax.ppermute(stamped, "grp", mate)
    other_wanted = other_stamped[:, fanout, 0]

    def candidate(target):
        here, there = wanted == target, other_wanted == target
        at_here = jnp.sum(jnp.where(here, jnp.arange(slot_count), 0))
        at_there = jnp.sum(jnp.where(there, jnp.arange(slot_count), 0))
        ours = jnp.any(here)
        pick = lambda a, b: jnp.where(
            ours,
            lax.dynamic_index_in_dim(a, at_here, 0, keepdims=False),
            lax.dynamic_index_in_dim(b, at_there, 0, keepdims=False),
        )
        return ours | jnp.any(there), pick(tiles, other_tiles), pick(stamped, other_stamped)

    held, points, stamps = candidate(me)
    for r in range(1, chips):
        target = ((place_x + r) % chips) * CORES + core
        _, points_out, stamps_out = candidate(target)
        over = [
            (x * CORES + c, ((x + r) % chips) * CORES + c)
            for x in range(chips)
            for c in range(CORES)
        ]
        points_in = lax.ppermute(points_out, "grp", over)
        stamps_in = lax.ppermute(stamps_out, "grp", over)
        take = stamps_in[fanout, 0] == me
        points = jnp.where(take, points_in, points)
        stamps = jnp.where(take, stamps_in, stamps)

    slots = owners * CAPACITY
    counter = jnp.arange(block_count)
    destination = targets // block_count
    same = destination[:, :, None] == destination[:, None, :]
    rank = jnp.sum(same & (counter[:, None] > counter[None, :]), axis=2)
    places = destination * CAPACITY + rank
    place = lax.dynamic_index_in_dim(places, mine, 0, keepdims=False)
    order = jnp.sum(
        jnp.where(place[None, :] == jnp.arange(slots)[:, None], counter[None, :], 0), axis=1
    ).astype(jnp.int32)
    sent_at = (jnp.arange(owners)[:, None] * CAPACITY + rank).reshape(-1)
    flat = targets.reshape(-1)
    goal = mine * block_count + counter
    fetch = jnp.sum(
        jnp.where(flat[None, :] == goal[:, None], sent_at[None, :], 0), axis=1
    ).astype(jnp.int32)
    back = jnp.sum(
        jnp.where(fetch[None, :] == jnp.arange(slots)[:, None], counter[None, :], 0), axis=1
    ).astype(jnp.int32)

    straight = jnp.arange(block_count, dtype=jnp.int32)
    section_one = run_block(
        points, stamps[:fanout] * (width // 128), first_params, straight, straight, rows, 16
    )
    outgoing = section_one.reshape(block_count, piece, width)[order].reshape(-1, width)
    swap = lambda a: lax.all_to_all(a, "dev", split_axis=0, concat_axis=0, tiled=True)
    incoming = swap(outgoing)
    section_two = run_block(
        incoming, neighbors_second * (width // 128), second_params, fetch, straight, rows, 16
    )
    backward = section_two.reshape(block_count, piece, width)[back].reshape(-1, width)
    returned = swap(backward).reshape(slots, piece, width)
    finished = returned[place].reshape(rows, width)

    gathered = [finished]
    for r in range(1, chips):
        over = [
            (x * CORES + c, ((x + r) % chips) * CORES + c)
            for x in range(chips)
            for c in range(CORES)
        ]
        gathered.append(lax.ppermute(finished, "grp", over))
    stack = jnp.stack(gathered)
    other = lax.ppermute(stack, "grp", mate)
    shift = (place_x - owner_group // CORES) % chips
    ours = owner_group % CORES == core
    parts = [
        jnp.where(
            filled[s],
            jnp.where(
                ours[s],
                lax.dynamic_index_in_dim(stack, shift[s], 0, keepdims=False),
                lax.dynamic_index_in_dim(other, shift[s], 0, keepdims=False),
            ),
            jnp.zeros((), jnp.bfloat16),
        )
        for s in range(slot_count)
    ]
    return jnp.concatenate(parts, axis=0)


def solution(mesh):
    return jax.shard_map(
        body,
        mesh=mesh,
        in_specs=(
            P(("grp", "dev"), None),
            P(("grp", "dev")),
            P(("grp", "dev")),
            P(None, ("grp", "dev")),
            P(("grp", "dev")),
            P(None, ("grp", "dev")),
            P(),
            P(),
            P(),
            P(),
            P(),
            P(),
            P(),
            P(),
            P(),
            P(),
        ),
        out_specs=P(("grp", "dev"), None),
        check_vma=False,
    )
```

```python
import functools
import math

import jax
import jax.numpy as jnp
from jax import lax
from jax.experimental import pallas as pl
from jax.experimental.pallas import tpu as pltpu
from jax.sharding import PartitionSpec as P

HEADS = 8
HEAD_DIM = 64
CAPACITY = 2
CORES = 2
CHUNK = 256
EPSILON = 1e-05
ONES = 16
TURNS = 4
QUARTERS = 4
LIMIT = 56 * 1024 * 1024


MESH = pl.DeviceIdType.MESH


def around(size, at, step):
    return lax.rem(at + step + size, size)


def greet(peers):
    barrier = pltpu.get_barrier_semaphore()
    for peer in peers:
        pl.semaphore_signal(barrier, inc=1, device_id=peer, device_id_type=MESH)
    return lambda: pl.semaphore_wait(barrier, len(peers))


def neighbours_of(groups, owners):
    me, mine = lax.axis_index("grp"), lax.axis_index("dev")
    chip, core = me // CORES, lax.rem(me, CORES)
    mate = (chip * CORES + 1 - core, mine)
    over = ((1 - chip) * CORES + core, mine)
    slant = ((1 - chip) * CORES + 1 - core, mine)
    return mate, over, slant


def owners_kernel(
    owners,
    points_ref,
    lists_ref,
    meta_ref,
    points_out,
    lists_out,
    metas_out,
    give_points,
    give_lists,
    mate_points,
    mate_lists,
    out_points,
    out_lists,
    in_points,
    in_lists,
    metas_ref,
    meta_send,
    meta_recv,
    mate_send,
    mate_recv,
    over_send,
    over_recv,
):
    me, mine = lax.axis_index("grp"), lax.axis_index("dev")
    rows = points_out.shape[0]
    part = rows // QUARTERS
    mate, over, slant = neighbours_of(4, owners)
    peers = [mate, over, slant] + [(me, around(owners, mine, k)) for k in range(1, owners)]
    entered = greet(peers)

    def flags(target):
        return [meta_ref[slot : slot + 1, :] == target for slot in range(2)]

    def chosen_points(target, q):
        one, two = [jnp.where(f, 1.0, 0.0).astype(jnp.bfloat16) for f in flags(target)]
        return (
            points_ref[pl.ds(q * part, part), :] * one
            + points_ref[pl.ds(rows + q * part, part), :] * two
        )

    def chosen_lists(target):
        one, two = [
            jnp.concatenate([jnp.where(f, 1, 0)] * (rows // f.shape[1]), axis=1)
            for f in flags(target)
        ]
        return lists_ref[:, :rows] * one + lists_ref[:, rows:] * two

    def copy(source, landing, send, recv, i, device):
        return pltpu.make_async_remote_copy(
            source, landing, send.at[i], recv.at[i], device_id=device, device_id_type=MESH
        )

    metas = [
        copy(meta_ref, metas_ref.at[i if i < 3 else i + 1], meta_send, meta_recv, i, peer)
        for i, peer in enumerate(peers)
    ]
    spans = [pl.ds(q * part, part) for q in range(QUARTERS)]
    gives = [
        [
            copy(
                give_points.at[half, span],
                mate_points.at[half, span],
                mate_send,
                mate_recv,
                half * QUARTERS + q,
                mate,
            )
            for q, span in enumerate(spans)
        ]
        + [
            copy(
                give_lists.at[half],
                mate_lists.at[half],
                mate_send,
                mate_recv,
                2 * QUARTERS + half,
                mate,
            )
        ]
        for half in range(2)
    ]
    sends = [
        copy(out_points.at[span], in_points.at[span], over_send, over_recv, q, over)
        for q, span in enumerate(spans)
    ] + [copy(out_lists, in_lists, over_send, over_recv, QUARTERS, over)]

    entered()
    for q, span in enumerate(spans):
        give_points[0, span] = chosen_points(slant[0], q)
        gives[0][q].start()
    give_lists[0] = chosen_lists(slant[0])
    gives[0][QUARTERS].start()
    for move in metas:
        move.start()
    metas_ref[3] = meta_ref[...]
    for q, span in enumerate(spans):
        kept = chosen_points(over[0], q)
        gives[0][q].wait_recv()
        out_points[span, :] = kept + mate_points[0, span]
        sends[q].start()
    kept = chosen_lists(over[0])
    gives[0][QUARTERS].wait_recv()
    out_lists[...] = kept + mate_lists[0]
    sends[QUARTERS].start()
    for q, span in enumerate(spans):
        give_points[1, span] = chosen_points(mate[0], q)
        gives[1][q].start()
    give_lists[1] = chosen_lists(mate[0])
    gives[1][QUARTERS].start()
    for q, span in enumerate(spans):
        kept = chosen_points(me, q)
        gives[1][q].wait_recv()
        points_out[span, :] = kept + mate_points[1, span]
    kept = chosen_lists(me)
    gives[1][QUARTERS].wait_recv()
    kept = kept + mate_lists[1]
    for move in metas:
        move.wait_recv()
    metas_out[...] = metas_ref[...]
    for q, span in enumerate(spans):
        sends[q].wait_recv()
        points_out[span, :] = points_out[span, :] + in_points[span, :]
    sends[QUARTERS].wait_recv()
    lists_out[...] = (kept + in_lists[...]) * (points_ref.shape[1] // 128)
    for move in metas + gives[0] + gives[1] + sends:
        move.wait_send()


def to_owners(points, lists, meta, owners):
    rows, width = points.shape[0] // 2, points.shape[1]
    fanout = lists.shape[0]
    vmem = pl.BlockSpec(memory_space=pltpu.VMEM)
    count = owners + 2
    return pl.pallas_call(
        functools.partial(owners_kernel, owners),
        out_shape=(
            jax.ShapeDtypeStruct((rows, width), points.dtype),
            jax.ShapeDtypeStruct((fanout, rows), jnp.int32),
            jax.ShapeDtypeStruct((count + 1,) + meta.shape, jnp.int32),
        ),
        in_specs=[vmem] * 3,
        out_specs=(vmem,) * 3,
        scratch_shapes=[
            pltpu.VMEM((2, rows, width), points.dtype),
            pltpu.VMEM((2, fanout, rows), jnp.int32),
            pltpu.VMEM((2, rows, width), points.dtype),
            pltpu.VMEM((2, fanout, rows), jnp.int32),
            pltpu.VMEM((rows, width), points.dtype),
            pltpu.VMEM((fanout, rows), jnp.int32),
            pltpu.VMEM((rows, width), points.dtype),
            pltpu.VMEM((fanout, rows), jnp.int32),
            pltpu.VMEM((count + 1,) + meta.shape, jnp.int32),
            pltpu.SemaphoreType.DMA((count,)),
            pltpu.SemaphoreType.DMA((count,)),
            pltpu.SemaphoreType.DMA((2 * QUARTERS + 2,)),
            pltpu.SemaphoreType.DMA((2 * QUARTERS + 2,)),
            pltpu.SemaphoreType.DMA((QUARTERS + 1,)),
            pltpu.SemaphoreType.DMA((QUARTERS + 1,)),
        ],
        compiler_params=pltpu.CompilerParams(
            collective_id=0, has_side_effects=True, vmem_limit_bytes=56 * 1024 * 1024
        ),
        cost_estimate=pl.CostEstimate(flops=1 << 20, bytes_accessed=8 << 20, transcendentals=0),
        name="to_owners",
    )(points, lists, meta)


def encode_kernel(
    products,
    cuts,
    fetch_ref,
    order_ref,
    near_ref,
    source_ref,
    lists_ref,
    depth_ref,
    features_ref,
    encoded_ref,
    x_ref,
    xt_ref,
    fine_ref,
    slim_ref,
    sums_ref,
    wide_ref,
    acc_ref,
    code_ref,
    tall_ref,
):
    rows, width = x_ref.shape
    fanout = depth_ref.shape[0]
    in_blocks = fetch_ref.shape[0]
    piece = rows // in_blocks
    chunks = rows // CHUNK
    lanes = 128
    parts = width // lanes
    for b in range(in_blocks):
        x_ref[pl.ds(b * piece, piece), :] = source_ref[
            pl.ds(pl.multiple_of(fetch_ref[b] * piece, piece), piece), :
        ]
    xt_ref[...] = x_ref[...].T
    for c in range(parts):
        fine_ref[pl.ds(c, rows, stride=parts), :] = x_ref[:, c * lanes : (c + 1) * lanes].astype(
            jnp.float32
        )
        slim_ref[pl.ds(c, fanout, stride=parts), :] = depth_ref[:, c * lanes : (c + 1) * lanes]
    tall_ref[...] = jnp.zeros_like(tall_ref)
    tall_ref[:fanout, :] = depth_ref[...]
    turned = tall_ref[...].T
    for j in range(products):
        wide_ref[j] = jnp.broadcast_to(turned[:, j : j + 1], (width, lanes))
    places = (lax.broadcasted_iota(jnp.int32, (rows, CHUNK), 0) * parts).astype(jnp.int16)
    one, nil = jnp.bfloat16(1), jnp.bfloat16(0)
    step = products // TURNS
    points = CHUNK // TURNS

    @pl.loop(0, chunks)
    def _(c):
        at = pl.multiple_of(c * CHUNK, CHUNK)
        acc_ref[...] = jnp.zeros_like(acc_ref)

        @pl.loop(0, TURNS)
        def _(t):
            first = t * points
            base = (c * TURNS + t) * (fanout * points)
            weights = [slim_ref[pl.ds(j * parts, parts), :] for j in range(products, fanout)]
            pieces = step * cuts
            deep = rows // cuts
            for i in range(pieces):
                j = t * step + i // cuts
                span = slice(i % cuts * deep, (i % cuts + 1) * deep)
                row = lists_ref[pl.ds(j, 1), pl.ds(at, CHUNK)].astype(jnp.int16)
                hot = jnp.where(places[span] == row, one, nil)
                got = jnp.dot(xt_ref[:, span], hot, preferred_element_type=jnp.float32)
                weight = wide_ref[j]
                acc_ref[...] += got * jnp.concatenate([weight] * (CHUNK // lanes), axis=1)
                for p in range(i * points // pieces, (i + 1) * points // pieces):
                    total = None
                    for near in range(products, fanout):
                        line = pl.multiple_of(near_ref[base + (near * points + p)], parts)
                        term = fine_ref[pl.ds(line, parts), :] * weights[near - products]
                        total = term if total is None else total + term
                    sums_ref[pl.ds(pl.multiple_of((first + p) * parts, parts), parts), :] = total

        for i in range(parts):
            code_ref[pl.ds(at, CHUNK), i * lanes : (i + 1) * lanes] = (
                acc_ref[i * lanes : (i + 1) * lanes, :].T
                + sums_ref[pl.ds(i, CHUNK, stride=parts), :]
            ).astype(jnp.bfloat16)

    for b in range(in_blocks):
        here = pl.ds(pl.multiple_of(order_ref[b] * piece, piece), piece)
        features_ref[pl.ds(b * piece, piece), :] = x_ref[here, :]
        encoded_ref[pl.ds(b * piece, piece), :] = code_ref[here, :]


def attention_kernel(
    mode,
    owners,
    x_ref,
    code_ref,
    mixing_ref,
    gain_ref,
    qkv_ref,
    out_w_ref,
    out_ref,
    updated_ref,
    qt_ref,
    k_ref,
    vt_ref,
    mixed_ref,
    result_ref,
    *extra,
):
    rows, width = x_ref.shape
    lanes = 128
    chunks = rows // CHUNK
    if mode != "alone":
        me, mine = lax.axis_index("grp"), lax.axis_index("dev")
        landed_ref, turn_send, turn_recv = extra[:3]
        peers = [(me, around(owners, mine, k)) for k in range(1, owners)]
        if mode == "home":
            mate, over, _ = neighbours_of(4, owners)
            peers += [mate, over]
        entered = greet(peers)
    gain = gain_ref[...]
    scale = HEAD_DIM**-0.5 * math.log2(math.e)

    @pl.loop(0, chunks)
    def _(c):
        here = pl.ds(pl.multiple_of(c * CHUNK, CHUNK), CHUNK)

        updated = x_ref[here, :].astype(jnp.float32) + jnp.dot(
            code_ref[here, :], mixing_ref[...], preferred_element_type=jnp.float32
        )
        updated_ref[here, :] = updated
        centre = jnp.mean(updated, axis=-1, keepdims=True)
        moved = updated - centre
        spread = jnp.mean(moved * moved, axis=-1, keepdims=True)
        normed = (moved * lax.rsqrt(spread + EPSILON) * gain).astype(jnp.bfloat16)
        project = jnp.dot(normed, qkv_ref[...], preferred_element_type=jnp.float32)
        qt_ref[:, here] = (project[:, :width] * scale).T.astype(jnp.bfloat16)
        k_ref[here, :] = project[:, width : 2 * width].astype(jnp.bfloat16)
        values = project[:, 2 * width :].T.astype(jnp.bfloat16)
        for h in range(HEADS):
            vt_ref[h, :HEAD_DIM, here] = values[h * HEAD_DIM : (h + 1) * HEAD_DIM]

    vt_ref[:, HEAD_DIM:, :] = jnp.ones((HEADS, ONES, rows), jnp.bfloat16)

    if mode != "alone":
        share = rows // owners

        def outgoing(k):
            return pltpu.make_async_remote_copy(
                result_ref.at[pl.ds(pl.multiple_of(k * share, share), share)],
                landed_ref.at[pl.ds(pl.multiple_of(mine * share, share), share)],
                turn_send.at[k],
                turn_recv.at[k],
                device_id=(me, around(owners, mine, k)),
                device_id_type=MESH,
            )

        def arriving(k):
            return pltpu.make_async_remote_copy(
                result_ref.at[pl.ds(pl.multiple_of(k * share, share), share)],
                landed_ref.at[
                    pl.ds(pl.multiple_of(around(owners, mine, -k) * share, share), share)
                ],
                turn_send.at[k],
                turn_recv.at[k],
                device_id=(me, around(owners, mine, k)),
                device_id_type=MESH,
            )

        if mode == "home":
            over_send, over_recv, own_send, own_recv, far_send, far_recv = extra[3:]

        def onward(k, source, landing, send, recv, device):
            at = pl.multiple_of(around(owners, mine, -k) * share, share)
            return pltpu.make_async_remote_copy(
                landed_ref.at[pl.ds(source * rows + at, share)],
                landed_ref.at[pl.ds(landing * rows + at, share)],
                send.at[k],
                recv.at[k],
                device_id=device,
                device_id_type=MESH,
            )

        def to_over(k):
            return onward(k, 0, 1, over_send, over_recv, over)

        def to_mate(k):
            return onward(k, 0, 2, own_send, own_recv, mate)

        def far_to_mate(k):
            return onward(k, 1, 3, far_send, far_recv, mate)

        def forward(k):
            arriving(k).wait_recv()
            to_over(k).start()
            to_mate(k).start()

        each = CHUNK // share
        entered()

    @pl.loop(0, chunks)
    def _(c):
        here = pl.ds(pl.multiple_of(c * CHUNK, CHUNK), CHUNK)

        def scored(h):
            pair = h // 2
            zero = jnp.zeros((HEAD_DIM, CHUNK), jnp.bfloat16)
            query = qt_ref[pl.ds(h * HEAD_DIM, HEAD_DIM), here]
            padded = jnp.concatenate([query, zero] if h % 2 == 0 else [zero, query], axis=0)
            return jnp.dot(
                k_ref[:, pair * lanes : (pair + 1) * lanes],
                padded,
                preferred_element_type=jnp.float32,
            )

        scores = scored(0)
        for h in range(HEADS):
            following = scored(h + 1) if h + 1 < HEADS else None
            peak = jnp.max(scores, axis=0, keepdims=True)
            powers = jnp.exp2(scores - peak).astype(jnp.bfloat16)
            mixed = jnp.dot(vt_ref[h], powers, preferred_element_type=jnp.float32)
            mixed_ref[pl.ds(h * HEAD_DIM, HEAD_DIM), :] = (
                mixed[:HEAD_DIM] / mixed[HEAD_DIM : HEAD_DIM + 1]
            )
            scores = following
        mixed = mixed_ref[...].T.astype(jnp.bfloat16)
        result_ref[here, :] = (
            updated_ref[here, :]
            + jnp.dot(mixed, out_w_ref[...], preferred_element_type=jnp.float32)
        ).astype(jnp.bfloat16)
        if mode == "alone":
            return

        @pl.when(c == 0)
        def _():
            landed_ref[pl.ds(pl.multiple_of(mine * share, share), share), :] = result_ref[
                pl.ds(0, share), :
            ]
            for k in range(1, each):
                outgoing(k).start()
            if mode == "home":
                to_over(0).start()
                to_mate(0).start()

        @pl.when(c > 0)
        def _():
            for i in range(each):
                outgoing(c * each + i).start()

        if mode == "home":

            @pl.when(c == 1)
            def _():
                for k in range(1, each):
                    forward(k)

            @pl.when(c > 1)
            def _():
                for i in range(each):
                    forward((c - 1) * each + i)

    if mode == "alone":
        out_ref[...] = result_ref[...]
        return
    if mode == "regroup":
        for k in range(1, owners):
            arriving(k).wait_recv()
        out_ref[...] = landed_ref[...]
        for k in range(1, owners):
            outgoing(k).wait_send()
        return

    done = 0
    for k in range(owners - each, owners):
        while done < k - 2:
            to_over(done).wait_recv()
            far_to_mate(done).start()
            done += 1
        forward(k)
    for k in range(done, owners):
        to_over(k).wait_recv()
        far_to_mate(k).start()
    for k in range(owners):
        to_mate(k).wait_recv()
        far_to_mate(k).wait_recv()
    out_ref[...] = landed_ref[...]
    for k in range(owners):
        to_over(k).wait_send()
        to_mate(k).wait_send()
        far_to_mate(k).wait_send()
    for k in range(1, owners):
        outgoing(k).wait_send()


def place_kernel(home_ref, source_ref, out_ref):
    pieces = home_ref.shape[0]
    piece = out_ref.shape[0] // pieces
    last = source_ref.shape[0] // piece
    for b in range(pieces):
        live = home_ref[b] < last
        here = pl.multiple_of(jnp.minimum(home_ref[b], last - 1) * piece, piece)
        found = source_ref[pl.ds(here, piece), :]
        out_ref[pl.ds(b * piece, piece), :] = jnp.where(live, found, jnp.zeros_like(found))


def put_home(source, home, piece):
    vmem = pl.BlockSpec(memory_space=pltpu.VMEM)
    return pl.pallas_call(
        place_kernel,
        out_shape=jax.ShapeDtypeStruct((home.shape[0] * piece, source.shape[1]), source.dtype),
        in_specs=[pl.BlockSpec(memory_space=pltpu.SMEM), vmem],
        out_specs=vmem,
        compiler_params=pltpu.CompilerParams(vmem_limit_bytes=LIMIT),
        name="put_home",
    )(home, source)


def run_block(source, lines, params, fetch, order, rows, products, cuts, mode="alone", owners=1):
    depth, mixing, gain, w_qkv, w_out = params
    width = source.shape[1]
    fanout = lines.shape[0]
    parts = width // 128
    vmem = pl.BlockSpec(memory_space=pltpu.VMEM)
    smem = pl.BlockSpec(memory_space=pltpu.SMEM)
    patch = jax.ShapeDtypeStruct((rows, width), jnp.bfloat16)
    near = lines.reshape(fanout, -1, CHUNK // TURNS).transpose(1, 0, 2).reshape(-1)
    features, encoded = pl.pallas_call(
        functools.partial(encode_kernel, products, cuts),
        out_shape=(patch, patch),
        in_specs=[smem] * 3 + [vmem] * 3,
        out_specs=(vmem, vmem),
        scratch_shapes=[
            pltpu.VMEM((rows, width), jnp.bfloat16),
            pltpu.VMEM((width, rows), jnp.bfloat16),
            pltpu.VMEM((rows * parts, 128), jnp.float32),
            pltpu.VMEM((fanout * parts, 128), jnp.float32),
            pltpu.VMEM((CHUNK * parts, 128), jnp.float32),
            pltpu.VMEM((products, width, 128), jnp.float32),
            pltpu.VMEM((width, CHUNK), jnp.float32),
            pltpu.VMEM((rows, width), jnp.bfloat16),
            pltpu.VMEM((128, width), jnp.float32),
        ],
        compiler_params=pltpu.CompilerParams(vmem_limit_bytes=LIMIT),
        cost_estimate=pl.CostEstimate(
            flops=2 * fanout * rows * rows * width, bytes_accessed=4 << 20, transcendentals=0
        ),
        name="encode",
    )(fetch, order, near, source, lines, depth)
    extra = []
    settings = pltpu.CompilerParams(vmem_limit_bytes=LIMIT)
    copies = 4 if mode == "home" else 1
    if mode != "alone":
        extra = [
            pltpu.VMEM((copies * rows, width), jnp.bfloat16),
            pltpu.SemaphoreType.DMA((owners,)),
            pltpu.SemaphoreType.DMA((owners,)),
        ]
        settings = pltpu.CompilerParams(
            vmem_limit_bytes=LIMIT,
            collective_id=1 if mode == "regroup" else 2,
            has_side_effects=True,
        )
    if mode == "home":
        extra += [pltpu.SemaphoreType.DMA((owners,))] * 6
    return pl.pallas_call(
        functools.partial(attention_kernel, mode, owners),
        out_shape=jax.ShapeDtypeStruct((copies * rows, width), jnp.bfloat16),
        in_specs=[vmem] * 6,
        out_specs=vmem,
        scratch_shapes=[
            pltpu.VMEM((rows, width), jnp.float32),
            pltpu.VMEM((width, rows), jnp.bfloat16),
            pltpu.VMEM((rows, width), jnp.bfloat16),
            pltpu.VMEM((HEADS, HEAD_DIM + ONES, rows), jnp.bfloat16),
            pltpu.VMEM((width, CHUNK), jnp.float32),
            pltpu.VMEM((rows, width), jnp.bfloat16),
        ]
        + extra,
        compiler_params=settings,
        cost_estimate=pl.CostEstimate(
            flops=10 * rows * width * width, bytes_accessed=8 << 20, transcendentals=8 << 20
        ),
        name="attention_" + mode,
    )(features, encoded, mixing, gain.reshape(1, width), w_qkv, w_out)


def body(
    home_points,
    counts,
    owner_group,
    neighbors_home,
    hilbert_target,
    neighbors_second,
    depth_first,
    mixing_first,
    gain_first,
    w_qkv_first,
    w_out_first,
    depth_second,
    mixing_second,
    gain_second,
    w_qkv_second,
    w_out_second,
):
    groups = lax.axis_size("grp")
    owners = lax.axis_size("dev")
    chips = groups // CORES
    me = lax.axis_index("grp")
    place_x, core = me // CORES, me % CORES
    mine = lax.axis_index("dev")
    home_rows, width = home_points.shape
    slot_count = owner_group.shape[0]
    rows = home_rows // slot_count
    block_count = hilbert_target.shape[0]
    piece = rows // block_count
    fanout = neighbors_home.shape[0]
    mate = [(i, i ^ 1) for i in range(groups)]
    first_params = (depth_first, mixing_first, gain_first, w_qkv_first, w_out_first)
    second_params = (depth_second, mixing_second, gain_second, w_qkv_second, w_out_second)

    if chips == 2 and slot_count == 2 and owners * CAPACITY == block_count:
        filled = jnp.arange(slot_count) < counts[0]
        wanted = jnp.where(filled, owner_group, -1)
        meta = jnp.concatenate(
            [
                jnp.broadcast_to(wanted[:, None], (slot_count, width)),
                jnp.broadcast_to(
                    jnp.pad(hilbert_target, (0, width - block_count))[None], (6, width)
                ),
            ]
        ).astype(jnp.int32)
        points, lines, metas = to_owners(home_points, neighbors_home, meta, owners)
        counter = jnp.arange(block_count)

        def slot_places(table):
            aim = table // block_count
            same = aim[:, :, None] == aim[:, None, :]
            rank = jnp.sum(same & (counter[:, None] > counter[None, :]), axis=2)
            return aim, rank

        told = metas[:, slot_count, :block_count]
        aim, rank = slot_places(told)
        own_aim, own_rank = slot_places(hilbert_target[None])
        turn = ((own_aim[0] - mine) % owners) * CAPACITY + own_rank[0]
        order = jnp.sum(
            jnp.where(turn[None, :] == counter[:, None], counter[None, :], 0), axis=1
        ).astype(jnp.int32)
        straight = jnp.arange(block_count, dtype=jnp.int32)
        incoming = run_block(
            points, lines, first_params, straight, order, rows, 12, 4, "regroup", owners
        )
        sender = (mine - jnp.arange(owners)) % owners
        sent_at = (sender[:, None] * CAPACITY + rank[3:]).reshape(-1)
        goal = mine * block_count + counter
        fetch = jnp.sum(
            jnp.where(told[3:].reshape(-1)[None, :] == goal[:, None], sent_at[None, :], 0), axis=1
        ).astype(jnp.int32)
        wheel = (counter + mine * CAPACITY) % block_count
        back = jnp.sum(
            jnp.where(fetch[None, :] == wheel[:, None], counter[None, :], 0), axis=1
        ).astype(jnp.int32)
        places = aim * CAPACITY + rank
        places = jnp.stack([places[3], places[1], places[0], places[2]])
        buffer = (owner_group // CORES != place_x) + 2 * (owner_group % CORES != core)
        home = jnp.where(
            filled[:, None], buffer[:, None] * block_count + places[buffer], 4 * block_count
        )
        buffers = run_block(
            incoming,
            neighbors_second * (width // 128),
            second_params,
            fetch,
            back,
            rows,
            12,
            2,
            "home",
            owners,
        )
        return put_home(buffers, home.reshape(-1).astype(jnp.int32), piece)

    targets = lax.all_gather(hilbert_target, "dev", axis=0, tiled=True).reshape(
        owners, block_count
    )

    filled = jnp.arange(slot_count) < counts[0]
    wanted = jnp.where(filled, owner_group, -1)
    tiles = home_points.reshape(slot_count, rows, width)
    lists = jnp.transpose(neighbors_home.reshape(fanout, slot_count, rows), (1, 0, 2))
    stamped = jnp.concatenate(
        [lists, jnp.broadcast_to(wanted[:, None, None], (slot_count, 1, rows))], axis=1
    )
    other_tiles = lax.ppermute(tiles, "grp", mate)
    other_stamped = lax.ppermute(stamped, "grp", mate)
    other_wanted = other_stamped[:, fanout, 0]

    def candidate(target):
        here, there = wanted == target, other_wanted == target
        at_here = jnp.sum(jnp.where(here, jnp.arange(slot_count), 0))
        at_there = jnp.sum(jnp.where(there, jnp.arange(slot_count), 0))
        ours = jnp.any(here)
        pick = lambda a, b: jnp.where(
            ours,
            lax.dynamic_index_in_dim(a, at_here, 0, keepdims=False),
            lax.dynamic_index_in_dim(b, at_there, 0, keepdims=False),
        )
        return ours | jnp.any(there), pick(tiles, other_tiles), pick(stamped, other_stamped)

    held, points, stamps = candidate(me)
    for r in range(1, chips):
        target = ((place_x + r) % chips) * CORES + core
        _, points_out, stamps_out = candidate(target)
        over = [
            (x * CORES + c, ((x + r) % chips) * CORES + c)
            for x in range(chips)
            for c in range(CORES)
        ]
        points_in = lax.ppermute(points_out, "grp", over)
        stamps_in = lax.ppermute(stamps_out, "grp", over)
        take = stamps_in[fanout, 0] == me
        points = jnp.where(take, points_in, points)
        stamps = jnp.where(take, stamps_in, stamps)

    slots = owners * CAPACITY
    counter = jnp.arange(block_count)
    destination = targets // block_count
    same = destination[:, :, None] == destination[:, None, :]
    rank = jnp.sum(same & (counter[:, None] > counter[None, :]), axis=2)
    places = destination * CAPACITY + rank
    place = lax.dynamic_index_in_dim(places, mine, 0, keepdims=False)
    order = jnp.sum(
        jnp.where(place[None, :] == jnp.arange(slots)[:, None], counter[None, :], 0), axis=1
    ).astype(jnp.int32)
    sent_at = (jnp.arange(owners)[:, None] * CAPACITY + rank).reshape(-1)
    flat = targets.reshape(-1)
    goal = mine * block_count + counter
    fetch = jnp.sum(
        jnp.where(flat[None, :] == goal[:, None], sent_at[None, :], 0), axis=1
    ).astype(jnp.int32)
    back = jnp.sum(
        jnp.where(fetch[None, :] == jnp.arange(slots)[:, None], counter[None, :], 0), axis=1
    ).astype(jnp.int32)

    straight = jnp.arange(block_count, dtype=jnp.int32)
    section_one = run_block(
        points, stamps[:fanout] * (width // 128), first_params, straight, straight, rows, 12, 4
    )
    outgoing = section_one.reshape(block_count, piece, width)[order].reshape(-1, width)
    swap = lambda a: lax.all_to_all(a, "dev", split_axis=0, concat_axis=0, tiled=True)
    incoming = swap(outgoing)
    section_two = run_block(
        incoming, neighbors_second * (width // 128), second_params, fetch, straight, rows, 12, 4
    )
    backward = section_two.reshape(block_count, piece, width)[back].reshape(-1, width)
    returned = swap(backward).reshape(slots, piece, width)
    finished = returned[place].reshape(rows, width)

    gathered = [finished]
    for r in range(1, chips):
        over = [
            (x * CORES + c, ((x + r) % chips) * CORES + c)
            for x in range(chips)
            for c in range(CORES)
        ]
        gathered.append(lax.ppermute(finished, "grp", over))
    stack = jnp.stack(gathered)
    other = lax.ppermute(stack, "grp", mate)
    shift = (place_x - owner_group // CORES) % chips
    ours = owner_group % CORES == core
    parts = [
        jnp.where(
            filled[s],
            jnp.where(
                ours[s],
                lax.dynamic_index_in_dim(stack, shift[s], 0, keepdims=False),
                lax.dynamic_index_in_dim(other, shift[s], 0, keepdims=False),
            ),
            jnp.zeros((), jnp.bfloat16),
        )
        for s in range(slot_count)
    ]
    return jnp.concatenate(parts, axis=0)


def solution(mesh):
    return jax.shard_map(
        body,
        mesh=mesh,
        in_specs=(
            P(("grp", "dev"), None),
            P(("grp", "dev")),
            P(("grp", "dev")),
            P(None, ("grp", "dev")),
            P(("grp", "dev")),
            P(None, ("grp", "dev")),
            P(),
            P(),
            P(),
            P(),
            P(),
            P(),
            P(),
            P(),
            P(),
            P(),
        ),
        out_specs=P(("grp", "dev"), None),
        check_vma=False,
    )
```
